512 devices in a mesh: dp: 32 (over y, x), expert: 16 (over z, core).
Axes of the slice: x: 4, y: 8, z: 8, core: 2. Of those that a mesh axis runs over, the one named last changes fastest.
Arguments:
- tokens: bfloat16 [65536, 2048], P('dp', 'expert'), may hold values from -6 to 6
- cotangent: bfloat16 [65536, 2048], P('dp', 'expert'), may hold values from -6 to 6
- down_proj: bfloat16 [2048, 512], P('expert'), may hold values from -0.125 to 0.125
- up_proj: bfloat16 [512, 2048], P(None, 'expert'), may hold values from -0.25 to 0.25
- routes: int32 [65536, 4], P(('dp', 'expert')), may hold values from 0 to 15, all different within a row; in each aligned block of 128 rows (0 to 127, 128 to 255, ...) at most 40 rows name the same one
- gate_weights: float32 [65536, 4], P(('dp', 'expert')), may hold values from 0.2 to 1
- expert_in: bfloat16 [16, 512, 2688], P('expert', 'dp'), may hold values from -0.25 to 0.25
- expert_out: bfloat16 [16, 1344, 512], P('expert', 'dp'), may hold values from -0.15625 to 0.15625
Outputs:
- mixed: bfloat16 [65536, 2048], P('dp', 'expert')
- input_grad: bfloat16 [65536, 2048], P('dp', 'expert')
- down_grad: float32 [2048, 512], P('expert')
- up_grad: float32 [512, 2048], P(None, 'expert')
The draws below stay inside these ranges and needn't reach their ends.
Inputs may be any that keep to these rules, and one draw needn't show every extreme that they name: `routes`: the rows of one device name no expert more than 40 times, a bound that some block reaches.
All inputs are finite; a program needn't handle non-finite values.
Results may differ from the reference program's by a relative error of at most 0.034.
Values may be sent and summed in bfloat16 or wider, within the bound.
No kernel may reach another device: no remote copies, remote signals or barrier semaphores. Data moves between devices by JAX's collectives and lax.ppermute only.
A program may use at most 64 MiB of HBM per device.

```python
import math
import jax
import jax.numpy as jnp
import numpy as np
from jax import lax

D = 2048
LATENT = 512
HIDDEN_SIZE = 1344
TOPK = 4
TOK_DEV = 128
EXPERTS = 16
CAP = 40
SLOTS = 640
TOKENS = 65536
N_EXPERT = 16


def strengthened(values, own_key, source, target, blocks, factor):
    owner, partner = [(jnp.arange(values.shape[dim]) // (values.shape[dim] // blocks)).reshape([-1 if axis == dim else 1 for axis in range(values.ndim)]) for dim in (source, target)]
    chosen = jax.random.permutation(own_key, blocks)[partner]
    strong = (owner == chosen) | (owner == (partner + blocks // 2) % blocks)
    return jnp.where(strong, factor * values, values)


def shard_levels(stream_key, dims, pieces, least, largest):
    def one(dim, blocks):
        heights = jax.random.uniform(jax.random.fold_in(jax.random.fold_in(stream_key, 6), dim), (blocks,), jnp.float32, least / len(pieces), largest / len(pieces))
        return jnp.repeat(jnp.exp(heights), dims[dim] // blocks).reshape((-1,) + (1,) * (len(dims) - dim - 1))

    level = one(*pieces[0])
    for cut in pieces[1:]:
        level = level * one(*cut)
    return level


def routed_block(key, own, number, rows, count, top, most, skew):
    order = jax.random.permutation(key, count)
    packed, common = shares(count, rows * top, most, skew, True), shares(count, rows * top, most, skew, False)
    places = jnp.arange(count)

    def named(lengths, rotation):
        used = int((lengths > 0).sum())
        fixed = max(1, used // 4)
        passed = fixed + (places - fixed + rotation * (used - fixed)) % max(1, count - fixed)
        return jnp.zeros((count,), jnp.int32).at[order[jnp.where(places < fixed, places, passed)]].set(jnp.asarray(lengths, jnp.int32))

    lengths = jnp.where(number % 4 == 0, named(packed, number // 4), named(common, number - number // 4 - 1))
    mixed = jax.random.permutation(jax.random.fold_in(own, 3), count)
    donor, taker = mixed[0:count // 2 * 2:2], mixed[1:count // 2 * 2:2]
    slack = jnp.minimum(lengths[donor] - 1, most - lengths[taker]) // 2
    slack = jnp.where((donor == order[0]) | (taker == order[0]) | (lengths[taker] == 0), 0, jnp.maximum(slack, 0))
    passed = jax.random.randint(jax.random.fold_in(own, 4), (count // 2,), 0, 1 << 20) % (slack + 1)
    lengths = lengths.at[donor].add(-passed).at[taker].add(passed)
    labels = jnp.searchsorted(jnp.cumsum(lengths), jnp.arange(rows * top), side="right").astype(jnp.int32)
    table = labels.reshape(top, rows).T
    table = table[jax.random.permutation(jax.random.fold_in(own, 1), rows)]
    rotation = jax.random.randint(jax.random.fold_in(own, 2), (rows, 1), 0, top)
    return jnp.take_along_axis(table, (jnp.arange(top)[None, :] + rotation) % top, axis=1)


def shares(number_of, total, reach, slope, full):
    loads = [(1 << 20) // math.isqrt(rank ** slope) + 1 for rank in range(1, number_of + 1)]
    largest = reach if full else min(reach, max(-(-total // number_of), total * loads[0] // sum(loads)))
    least = 1 if total - largest >= number_of - 1 else 0
    counts, spare = [largest] + [least] * (number_of - 1), total - largest - least * (number_of - 1)
    while spare > 0:
        movable = [i for i in range(1, number_of) if counts[i] < largest] or [i for i in range(1, number_of) if counts[i] < reach]
        pool, budget = sum([loads[i] for i in movable]), spare
        for i in movable:
            addition = min(reach - counts[i], max(1, budget * loads[i] // pool), spare)
            counts[i] = counts[i] + addition
            spare = spare - addition
    return np.array(counts)


def gaussian(stream_key, dims, spread, bound, split=(), kind=jnp.bfloat16):
    entries = jax.random.normal(stream_key, dims, jnp.float32) * spread
    if len(split) > 0:
        entries = shard_levels(stream_key, dims, split, -0.22, 0.18) * entries
    return jnp.clip(entries, min=-bound, max=bound).astype(kind)


def noise_with(stream_key, dims, scale, most, cuts, heavy, kind=jnp.bfloat16):
    entries = scale * jax.random.normal(stream_key, dims, jnp.float32)
    if cuts:
        entries = entries * shard_levels(stream_key, dims, cuts, -0.22, 0.18)
    return jnp.clip(strengthened(entries, jax.random.fold_in(stream_key, 3), *heavy), -most, most).astype(kind)


def setup_inputs(seed: int = 0) -> dict:
    splits = jax.random.split(jax.random.key(seed), 9)
    tokens = noise_with(splits[0], (TOKENS, D), 1.0, 6.0, ((0, 32), (1, 16)), (1, 0, 32, 2.75))
    cotangent = noise_with(splits[1], (TOKENS, D), 1.0, 6.0, ((0, 32), (1, 16)), (1, 0, 32, 2.75))
    down_proj = gaussian(splits[2], (D, LATENT), D ** -0.5, 0.125, ((0, 16),))
    up_proj = gaussian(splits[3], (LATENT, D), LATENT ** -0.5, 0.25, ((1, 16),))
    routes_keys = jax.random.split(jax.random.fold_in(splits[4], 1), TOKENS // TOK_DEV)
    routes_turns = jax.random.permutation(jax.random.fold_in(splits[4], 3), TOKENS // TOK_DEV)
    routes = jax.vmap(lambda own, number: routed_block(jax.random.fold_in(splits[4], 2), own, number, TOK_DEV, EXPERTS, TOPK, CAP, 2))(routes_keys, routes_turns).reshape((TOKENS, TOPK))
    gate_weights = jnp.clip(0.2 + 0.8 * jax.random.uniform(splits[5], (TOKENS, TOPK), jnp.float32) ** shard_levels(splits[5], (TOKENS, TOPK), ((0, 512),), -0.2, 0.2), 0.2, 1.0)
    expert_in = gaussian(splits[6], (EXPERTS, LATENT, 2 * HIDDEN_SIZE), LATENT ** -0.5, 0.25, ((0, 16), (1, 32)))
    expert_out = gaussian(splits[7], (EXPERTS, HIDDEN_SIZE, LATENT), HIDDEN_SIZE ** -0.5, 0.15625, ((0, 16), (1, 32)))
    return dict(tokens=tokens, cotangent=cotangent, down_proj=down_proj, up_proj=up_proj, routes=routes, gate_weights=gate_weights, expert_in=expert_in, expert_out=expert_out)


def swiglu_forward(pre_act, hidden):
    gate_part = pre_act[:, :hidden]
    up_part = pre_act[:, hidden:]
    return gate_part * jax.nn.sigmoid(gate_part) * up_part

def swiglu_backward(pre_act, grad_act, hidden):
    gate_part = pre_act[:, :hidden]
    up_part = pre_act[:, hidden:]
    sigmoid_gate = jax.nn.sigmoid(gate_part)
    grad_gate = grad_act * up_part * sigmoid_gate * (1.0 + gate_part * (1.0 - sigmoid_gate))
    grad_upper = grad_act * (gate_part * sigmoid_gate)
    return jnp.concatenate([grad_gate, grad_upper], axis=1)

def block_sum(left, right):
    width = left.shape[1] // N_EXPERT
    left_blocks = left.reshape(left.shape[0], N_EXPERT, width).transpose(1, 0, 2)
    right_blocks = right.reshape(N_EXPERT, width, right.shape[1])

    def accumulate(running, pair):
        part = jnp.dot(pair[0], pair[1], preferred_element_type=jnp.float32).astype(jnp.bfloat16)
        part = lax.optimization_barrier(part)
        return (running + part.astype(jnp.float32), None)
    start_value = jnp.zeros((left.shape[0], right.shape[1]), jnp.float32)
    summed, unused = lax.scan(accumulate, start_value, (left_blocks, right_blocks))
    return summed.astype(jnp.bfloat16)

def reference(tokens, cotangent, down_proj, up_proj, routes, gate_weights, expert_in, expert_out):
    block_count = TOKENS // TOK_DEV
    pair_count = TOK_DEV * TOPK
    latent = block_sum(tokens, down_proj)
    latent_out_grad = block_sum(cotangent, up_proj.T)
    block_routes = routes.reshape(block_count, pair_count)
    onehot = (block_routes[:, :, None] == jnp.arange(EXPERTS, dtype=jnp.int32)[None, None, :]).astype(jnp.int32)
    before = jnp.cumsum(onehot, axis=1) - onehot
    position = lax.optimization_barrier(jnp.sum(before * onehot, axis=2))
    slot = (block_routes * CAP + position).astype(jnp.int32)
    block_ids = jnp.broadcast_to(jnp.arange(block_count, dtype=jnp.int32)[:, None], (block_count, pair_count))
    latent_pairs = jnp.broadcast_to(latent.reshape(TOKENS, 1, LATENT), (TOKENS, TOPK, LATENT)).reshape(block_count, pair_count, LATENT)
    dispatched = jnp.zeros((block_count, SLOTS, LATENT), jnp.bfloat16).at[block_ids, slot].set(latent_pairs)
    gated = (gate_weights[:, :, None] * latent_out_grad.astype(jnp.float32)[:, None, :]).astype(jnp.bfloat16)
    routed_grad = jnp.zeros((block_count, SLOTS, LATENT), jnp.bfloat16).at[block_ids, slot].set(gated.reshape(block_count, pair_count, LATENT))

    def per_expert(array):
        return array.reshape(block_count, EXPERTS, CAP, LATENT).transpose(1, 0, 2, 3).reshape(EXPERTS, block_count * CAP, LATENT)

    def from_expert(array):
        return array.reshape(EXPERTS, block_count, CAP, LATENT).transpose(1, 0, 2, 3).reshape(block_count, SLOTS, LATENT)

    def expert_step(operands):
        rows_in, grad_rows_in, weight_in, weight_out = operands
        pre_act = jnp.dot(rows_in, weight_in, preferred_element_type=jnp.float32)
        activation = swiglu_forward(pre_act, HIDDEN_SIZE).astype(jnp.bfloat16)
        rows_out = jnp.dot(activation, weight_out, preferred_element_type=jnp.float32).astype(jnp.bfloat16)
        grad_act = lax.dot_general(grad_rows_in, weight_out, (((1,), (1,)), ((), ())), preferred_element_type=jnp.float32)
        grad_pre = swiglu_backward(pre_act, grad_act, HIDDEN_SIZE).astype(jnp.bfloat16)
        grad_rows_out = lax.dot_general(grad_pre, weight_in, (((1,), (1,)), ((), ())), preferred_element_type=jnp.float32).astype(jnp.bfloat16)
        return (rows_out, grad_rows_out)
    expert_rows, rows_grad = lax.map(expert_step, (per_expert(dispatched), per_expert(routed_grad), expert_in, expert_out))
    expert_rows = from_expert(expert_rows)
    rows_grad = from_expert(rows_grad)
    picked = jnp.take_along_axis(expert_rows, slot[:, :, None], axis=1).astype(jnp.float32).reshape(TOKENS, TOPK, LATENT)
    latent_out = lax.optimization_barrier(jnp.sum(picked * gate_weights[:, :, None], axis=1)).astype(jnp.bfloat16)
    picked_grad = jnp.take_along_axis(rows_grad, slot[:, :, None], axis=1).astype(jnp.float32).reshape(TOKENS, TOPK, LATENT)
    latent_grad = lax.optimization_barrier(jnp.sum(picked_grad, axis=1)).astype(jnp.bfloat16)
    grad_scale = 1.0 / math.sqrt(TOKENS)
    mixed = jnp.dot(latent_out, up_proj, preferred_element_type=jnp.float32).astype(jnp.bfloat16)
    up_grad = lax.dot_general(latent_out, cotangent, (((0,), (0,)), ((), ())), preferred_element_type=jnp.float32) * grad_scale
    input_grad = lax.dot_general(latent_grad, down_proj, (((1,), (1,)), ((), ())), preferred_element_type=jnp.float32).astype(jnp.bfloat16)
    down_grad = lax.dot_general(tokens, latent_grad, (((0,), (0,)), ((), ())), preferred_element_type=jnp.float32) * grad_scale
    return (mixed, input_grad, down_grad, up_grad)
```

```python
import math

import jax
import jax.numpy as jnp
from jax import lax
from jax.sharding import Mesh
from jax.sharding import PartitionSpec as P

TOPK = 4
CORES = 2
COLS = (((1,), (1,)), ((), ()))
ROWS = (((0,), (0,)), ((), ()))


def dot(left, right, dims=(((1,), (0,)), ((), ()))):
    return lax.dot_general(left, right, dims, preferred_element_type=jnp.float32)


def slot_tables(routes, gate_weights, experts, capacity):
    flat_routes = routes.reshape(-1)
    onehot = (flat_routes[:, None] == jnp.arange(experts, dtype=jnp.int32)[None, :]).astype(
        jnp.int32
    )
    before = jnp.cumsum(onehot, axis=0) - onehot
    position = jnp.sum(before * onehot, axis=1)
    slot = (flat_routes * capacity + position).reshape(routes.shape)
    slot_ids = jnp.arange(experts * capacity, dtype=jnp.int32)
    matches = slot.T[:, None, :] == slot_ids[None, :, None]
    spread = jnp.any(matches, axis=0)
    weighted = jnp.sum(jnp.where(matches, gate_weights.T[:, None, :], 0.0), axis=0)
    return spread.astype(jnp.bfloat16), weighted


def on_device(tokens, cotangent, down_proj, up_proj, routes, gate_weights, expert_in, expert_out):
    chips = lax.axis_size("z")
    groups = chips * CORES
    dp = lax.axis_size("dp")
    core = lax.axis_index("c")
    tok_rows = routes.shape[0]
    group_rows = tokens.shape[0]
    features = tokens.shape[1]
    latent_width = down_proj.shape[1]
    hidden = expert_in.shape[2] // 2
    capacity = min(tok_rows, tok_rows * TOPK * 5 // (4 * groups))
    slot_count = groups * capacity
    grad_scale = 1.0 / math.sqrt(group_rows * dp)
    bf16 = jnp.bfloat16

    weight_in = lax.all_gather(expert_in, "dp", axis=1, tiled=True)[0]
    weight_out = lax.all_gather(expert_out, "dp", axis=1, tiled=True)[0]

    swap = [(0, 1), (1, 0)]

    def halves(array):
        blocks = array.reshape(chips, CORES, tok_rows, features)
        kept = lax.dynamic_index_in_dim(blocks, core, 1, keepdims=False)
        given = lax.dynamic_index_in_dim(blocks, 1 - core, 1, keepdims=False)
        got = lax.ppermute(given, "c", swap)
        return jnp.concatenate([kept, got], axis=2).reshape(chips * tok_rows, CORES * features)

    down_both = jnp.concatenate([down_proj, lax.ppermute(down_proj, "c", swap)], axis=0)
    up_both = jnp.concatenate([up_proj, lax.ppermute(up_proj, "c", swap)], axis=1)
    part = dot(halves(tokens), down_both).astype(bf16)
    part_grad = dot(halves(cotangent), up_both, COLS).astype(bf16)
    parts = jnp.concatenate([part, part_grad], axis=1).reshape(chips, tok_rows, 2 * latent_width)
    parts = lax.all_to_all(parts, "z", split_axis=0, concat_axis=0, tiled=True)
    latents = jnp.sum(parts.astype(jnp.float32), axis=0).astype(bf16)

    spread, weighted = slot_tables(routes, gate_weights, groups, capacity)
    slot_gate = jnp.sum(weighted, axis=1, keepdims=True)
    gate_high = weighted.astype(bf16)
    gate_low = (weighted - gate_high.astype(jnp.float32)).astype(bf16)

    outgoing = dot(spread, latents)
    outgoing = jnp.concatenate(
        [outgoing[:, :latent_width], outgoing[:, latent_width:] * slot_gate], axis=1
    ).astype(bf16)

    def exchange(rows):
        return lax.all_to_all(
            rows.reshape(groups, capacity, 2 * latent_width),
            ("z", "c"),
            split_axis=0,
            concat_axis=0,
            tiled=True,
        ).reshape(slot_count, 2 * latent_width)

    received = exchange(outgoing)
    pre_act = dot(received[:, :latent_width], weight_in)
    gate_part = pre_act[:, :hidden]
    up_part = pre_act[:, hidden:]
    sigmoid_gate = jax.nn.sigmoid(gate_part)
    silu = gate_part * sigmoid_gate
    rows_out = dot((silu * up_part).astype(bf16), weight_out).astype(bf16)
    grad_act = dot(received[:, latent_width:], weight_out, COLS)
    grad_gate = grad_act * up_part * sigmoid_gate * (1.0 + gate_part * (1.0 - sigmoid_gate))
    grad_upper = grad_act * silu
    pre_grad = jnp.concatenate([grad_gate, grad_upper], axis=1).astype(bf16)
    rows_grad = dot(pre_grad, weight_in, COLS).astype(bf16)
    returned = exchange(jnp.concatenate([rows_out, rows_grad], axis=1))
    returned_out = returned[:, :latent_width]
    latent_out = (dot(gate_high, returned_out, ROWS) + dot(gate_low, returned_out, ROWS)).astype(
        bf16
    )
    latent_grad = dot(spread, returned[:, latent_width:], ROWS).astype(bf16)

    all_out = lax.all_gather(latent_out, ("z", "c"), axis=0, tiled=True)
    all_grad = lax.all_gather(latent_grad, ("z", "c"), axis=0, tiled=True)
    mixed = dot(all_out, up_proj).astype(bf16)
    input_grad = dot(all_grad, down_proj, COLS).astype(bf16)
    up_part_grad = dot(all_out, cotangent, ROWS)
    down_part_grad = dot(all_grad, tokens, ROWS)
    grads = jnp.concatenate([up_part_grad, down_part_grad], axis=1).astype(bf16)
    grads = grads.reshape(dp, latent_width // dp, 2 * features)
    grads = lax.all_to_all(grads, "dp", split_axis=0, concat_axis=0, tiled=True)
    summed = jnp.sum(grads.astype(jnp.float32), axis=0).astype(bf16)
    summed = jnp.broadcast_to(summed[None], grads.shape)
    summed = lax.all_to_all(summed, "dp", split_axis=0, concat_axis=0, tiled=True)
    summed = summed.reshape(latent_width, 2 * features).astype(jnp.float32) * grad_scale
    return mixed, input_grad, summed[:, features:].T, summed[:, :features]


def solution(mesh):
    dp, experts = mesh.devices.shape
    fine = Mesh(mesh.devices.reshape(dp, experts // CORES, CORES), ("dp", "z", "c"))
    expert = ("z", "c")
    in_specs = (
        P("dp", expert),
        P("dp", expert),
        P(expert, None),
        P(None, expert),
        P(("dp", "z", "c"), None),
        P(("dp", "z", "c"), None),
        P(expert, "dp", None),
        P(expert, "dp", None),
    )
    out_specs = (P("dp", expert), P("dp", expert), P(expert, None), P(None, expert))
    return jax.shard_map(
        on_device, mesh=fine, in_specs=in_specs, out_specs=out_specs, check_vma=False
    )
```

```python
import math

import jax
import jax.numpy as jnp
from jax import lax
from jax.experimental import pallas as pl
from jax.experimental.pallas import tpu as pltpu
from jax.sharding import Mesh
from jax.sharding import PartitionSpec as P

TOPK = 4
CORES = 2
CHUNK = 256
INNER = (((1,), (0,)), ((), ()))
COLS = (((1,), (1,)), ((), ()))
ROWS = (((0,), (0,)), ((), ()))


def dot(left, right, dims=INNER):
    return lax.dot_general(left, right, dims, preferred_element_type=jnp.float32)


def slot_tables(routes, gate_weights, experts, capacity):
    flat_routes = routes.reshape(-1)
    onehot = (flat_routes[:, None] == jnp.arange(experts, dtype=jnp.int32)[None, :]).astype(
        jnp.int32
    )
    before = jnp.cumsum(onehot, axis=0) - onehot
    position = jnp.sum(before * onehot, axis=1)
    slot = (flat_routes * capacity + position).reshape(routes.shape)
    slot_ids = jnp.arange(experts * capacity, dtype=jnp.int32)
    matches = slot.T[:, None, :] == slot_ids[None, :, None]
    spread = jnp.any(matches, axis=0)
    weighted = jnp.sum(jnp.where(matches, gate_weights.T[:, None, :], 0.0), axis=0)
    return spread.astype(jnp.bfloat16), weighted


def packed_weights(expert_in, expert_out, dp):
    in_rows, width = expert_in.shape[1:]
    own, latent_width = expert_out.shape[1:]
    hidden = width // 2
    tiles = -(-own // in_rows)
    place = jnp.arange(tiles * dp * in_rows, dtype=jnp.int32)
    tile, device, row = place // (dp * in_rows), place // in_rows % dp, place % in_rows
    unit = tile * in_rows + row
    source = jnp.where(unit < own, device * own + unit, -1)
    pick = (jnp.arange(hidden, dtype=jnp.int32)[:, None] == source[None, :]).astype(jnp.bfloat16)
    both = jnp.concatenate([expert_in[0, :, :hidden], expert_in[0, :, hidden:]], axis=0)
    both = dot(both, pick).astype(jnp.bfloat16)
    rows = jnp.pad(expert_out[0], ((0, tiles * in_rows - own), (0, 0)))
    rows = [rows[t * in_rows : (t + 1) * in_rows] for t in range(tiles)]
    return jnp.concatenate([both[:in_rows], both[in_rows:], *rows], axis=1)


def expert_kernel(rows_ref, gate_ref, up_ref, out_ref, result_ref, sum_out, sum_grad):
    step = pl.program_id(0)
    latent_width = sum_out.shape[1]

    @pl.when(step == 0)
    def _():
        sum_out[...] = jnp.zeros_like(sum_out)
        sum_grad[...] = jnp.zeros_like(sum_grad)

    rows = rows_ref[:, :latent_width]
    gate_part = dot(rows, gate_ref[...])
    up_part = dot(rows, up_ref[...])
    grad_act = dot(rows_ref[:, latent_width:], out_ref[...], COLS)
    sigmoid_gate = jax.nn.sigmoid(gate_part)
    silu = gate_part * sigmoid_gate
    sum_out[...] += dot((silu * up_part).astype(jnp.bfloat16), out_ref[...])
    grad_gate = grad_act * up_part * sigmoid_gate * (1.0 + gate_part * (1.0 - sigmoid_gate))
    sum_grad[...] += dot(grad_gate.astype(jnp.bfloat16), gate_ref[...], COLS)
    sum_grad[...] += dot((grad_act * silu).astype(jnp.bfloat16), up_ref[...], COLS)

    @pl.when(step == pl.num_programs(0) - 1)
    def _():
        result_ref[:, :latent_width] = sum_out[...].astype(jnp.bfloat16)
        result_ref[:, latent_width:] = sum_grad[...].astype(jnp.bfloat16)


def run_expert(rows, weights):
    count, latent_width = rows.shape[0], rows.shape[1] // 2
    padded = weights.shape[1] // 3
    steps = padded // CHUNK
    halves = latent_width // CHUNK
    out_base = 2 * padded // latent_width
    return pl.pallas_call(
        expert_kernel,
        grid=(steps,),
        in_specs=[
            pl.BlockSpec((count, 2 * latent_width), lambda j: (0, 0)),
            pl.BlockSpec((latent_width, CHUNK), lambda j: (0, j)),
            pl.BlockSpec((latent_width, CHUNK), lambda j: (0, steps + j)),
            pl.BlockSpec((CHUNK, latent_width), lambda j: (j % halves, out_base + j // halves)),
        ],
        out_specs=pl.BlockSpec((count, 2 * latent_width), lambda j: (0, 0)),
        out_shape=jax.ShapeDtypeStruct((count, 2 * latent_width), jnp.bfloat16),
        scratch_shapes=[pltpu.VMEM((count, latent_width), jnp.float32)] * 2,
        compiler_params=pltpu.CompilerParams(vmem_limit_bytes=32 * 1024 * 1024),
        cost_estimate=pl.CostEstimate(
            flops=12 * count * latent_width * padded,
            bytes_accessed=2 * (weights.size + 2 * rows.size),
            transcendentals=count * padded,
        ),
    )(rows, weights, weights, weights)


def on_device(tokens, cotangent, down_proj, up_proj, routes, gate_weights, expert_in, expert_out):
    expert = ("z", "c")
    chips = lax.axis_size("z")
    core = lax.axis_index("c")
    groups = chips * CORES
    dp = lax.axis_size("dp")
    tok_rows = routes.shape[0]
    group_rows = tokens.shape[0]
    features = tokens.shape[1]
    latent_width = down_proj.shape[1]
    capacity = min(tok_rows, tok_rows * TOPK * 5 // (4 * groups))
    slot_count = groups * capacity
    grad_scale = 1.0 / math.sqrt(group_rows * dp)
    bf16 = jnp.bfloat16

    swap = [(0, 1), (1, 0)]

    def partial_latent(rows, weights_here, column_dims):
        blocks = rows.reshape(chips, CORES, tok_rows, features)
        kept = lax.dynamic_index_in_dim(blocks, core, 1, keepdims=False)
        given = lax.dynamic_index_in_dim(blocks, 1 - core, 1, keepdims=False)
        got = lax.ppermute(given, "c", swap)
        weights_there = lax.ppermute(weights_here, "c", swap)
        kept = kept.reshape(chips * tok_rows, features)
        got = got.reshape(chips * tok_rows, features)
        part = dot(kept, weights_here, column_dims) + dot(got, weights_there, column_dims)
        return part.astype(bf16).reshape(chips, tok_rows, latent_width)

    weights = lax.all_gather(packed_weights(expert_in, expert_out, dp), "dp", axis=0, tiled=True)

    spread, weighted = slot_tables(routes, gate_weights, groups, capacity)
    slot_gate = jnp.sum(weighted, axis=1, keepdims=True)
    gate_high = weighted.astype(bf16)
    gate_low = (weighted - gate_high.astype(jnp.float32)).astype(bf16)

    def exchange(rows):
        return lax.all_to_all(
            rows.reshape(groups, capacity, rows.shape[1]),
            expert,
            split_axis=0,
            concat_axis=0,
            tiled=True,
        ).reshape(slot_count, rows.shape[1])

    latent = partial_latent(tokens, down_proj, INNER).reshape(chips * tok_rows, latent_width)
    latent = lax.psum_scatter(latent, "z", scatter_dimension=0, tiled=True)
    parts = partial_latent(cotangent, up_proj, COLS)
    parts = lax.all_to_all(parts, "z", split_axis=0, concat_axis=0, tiled=True)
    latent_out_grad = jnp.sum(parts.astype(jnp.float32), axis=0).astype(bf16)
    outgoing = [dot(spread, latent), dot(spread, latent_out_grad) * slot_gate]
    result = run_expert(exchange(jnp.concatenate(outgoing, axis=1).astype(bf16)), weights)
    returned = exchange(result)
    returned_out = returned[:, :latent_width]
    latent_out = (dot(gate_high, returned_out, ROWS) + dot(gate_low, returned_out, ROWS)).astype(
        bf16
    )
    latent_grad = dot(spread, returned[:, latent_width:], ROWS).astype(bf16)

    latents = jnp.concatenate([latent_out, latent_grad], axis=1)
    latents = lax.all_gather(latents, expert, axis=0, tiled=True)
    all_out = latents[:, :latent_width]
    all_grad = latents[:, latent_width:]
    up_part_grad = dot(all_out, cotangent, ROWS)
    down_part_grad = dot(all_grad, tokens, ROWS)
    grads = jnp.concatenate([up_part_grad, down_part_grad], axis=1).astype(bf16)
    grads = grads.reshape(dp, latent_width // dp, 2 * features)
    grads = lax.all_to_all(grads, "dp", split_axis=0, concat_axis=0, tiled=True)
    mixed = dot(all_out, up_proj).astype(bf16)
    input_grad = dot(all_grad, down_proj, COLS).astype(bf16)
    summed = jnp.sum(grads.astype(jnp.float32), axis=0).astype(bf16)
    summed = jnp.broadcast_to(summed[None], grads.shape)
    summed = lax.all_to_all(summed, "dp", split_axis=0, concat_axis=0, tiled=True)
    summed = summed.reshape(latent_width, 2 * features).astype(jnp.float32) * grad_scale
    return mixed, input_grad, summed[:, features:].T, summed[:, :features]


def solution(mesh):
    dp, experts = mesh.devices.shape
    fine = Mesh(mesh.devices.reshape(dp, experts // CORES, CORES), ("dp", "z", "c"))
    expert = ("z", "c")
    in_specs = (
        P("dp", expert),
        P("dp", expert),
        P(expert, None),
        P(None, expert),
        P(("dp", "z", "c"), None),
        P(("dp", "z", "c"), None),
        P(expert, "dp", None),
        P(expert, "dp", None),
    )
    out_specs = (P("dp", expert), P("dp", expert), P(expert, None), P(None, expert))
    return jax.shard_map(
        on_device, mesh=fine, in_specs=in_specs, out_specs=out_specs, check_vma=False
    )
```

```python
import functools
import math

import jax
import jax.numpy as jnp
from jax import lax
from jax.experimental import pallas as pl
from jax.experimental.pallas import tpu as pltpu
from jax.sharding import Mesh
from jax.sharding import PartitionSpec as P

TOPK = 4
CORES = 2
CHUNK = 256
SMALL = pltpu.CompilerParams(vmem_limit_bytes=16 * 1024 * 1024)
LARGE = pltpu.CompilerParams(vmem_limit_bytes=56 * 1024 * 1024)
INNER = (((1,), (0,)), ((), ()))
COLS = (((1,), (1,)), ((), ()))
ROWS = (((0,), (0,)), ((), ()))


def dot(left, right, dims=INNER):
    return lax.dot_general(left, right, dims, preferred_element_type=jnp.float32)


def slot_tables(routes, gate_weights, experts, capacity):
    flat_routes = routes.reshape(-1)
    onehot = (flat_routes[:, None] == jnp.arange(experts, dtype=jnp.int32)[None, :]).astype(
        jnp.int32
    )
    before = jnp.cumsum(onehot, axis=0) - onehot
    position = jnp.sum(before * onehot, axis=1)
    slot = (flat_routes * capacity + position).reshape(routes.shape)
    slot_ids = jnp.arange(experts * capacity, dtype=jnp.int32)
    matches = slot.T[:, None, :] == slot_ids[None, :, None]
    spread = jnp.any(matches, axis=0)
    weighted = jnp.sum(jnp.where(matches, gate_weights.T[:, None, :], 0.0), axis=0)
    return spread.astype(jnp.bfloat16), weighted


def packed_weights(expert_in, expert_out, dp):
    in_rows, width = expert_in.shape[1:]
    own, latent_width = expert_out.shape[1:]
    hidden = width // 2
    tiles = -(-own // in_rows)
    place = jnp.arange(tiles * dp * in_rows, dtype=jnp.int32)
    tile, device, row = place // (dp * in_rows), place // in_rows % dp, place % in_rows
    unit = tile * in_rows + row
    source = jnp.where(unit < own, device * own + unit, -1)
    pick = (jnp.arange(hidden, dtype=jnp.int32)[:, None] == source[None, :]).astype(jnp.bfloat16)
    both = jnp.concatenate([expert_in[0, :, :hidden], expert_in[0, :, hidden:]], axis=0)
    both = dot(both, pick).astype(jnp.bfloat16)
    rows = jnp.pad(expert_out[0], ((0, tiles * in_rows - own), (0, 0)))
    rows = [rows[t * in_rows : (t + 1) * in_rows] for t in range(tiles)]
    return jnp.concatenate([both[:in_rows], both[in_rows:], *rows], axis=1)


def expert_kernel(rows_ref, gate_ref, up_ref, out_ref, result_ref, sum_out, sum_grad):
    step = pl.program_id(0)
    latent_width = sum_out.shape[1]

    @pl.when(step == 0)
    def _():
        sum_out[...] = jnp.zeros_like(sum_out)
        sum_grad[...] = jnp.zeros_like(sum_grad)

    rows = rows_ref[:, :latent_width]
    gate_part = dot(rows, gate_ref[...])
    up_part = dot(rows, up_ref[...])
    grad_act = dot(rows_ref[:, latent_width:], out_ref[...], COLS)
    sigmoid_gate = jax.nn.sigmoid(gate_part)
    silu = gate_part * sigmoid_gate
    sum_out[...] += dot((silu * up_part).astype(jnp.bfloat16), out_ref[...])
    grad_gate = grad_act * up_part * sigmoid_gate * (1.0 + gate_part * (1.0 - sigmoid_gate))
    sum_grad[...] += dot(grad_gate.astype(jnp.bfloat16), gate_ref[...], COLS)
    sum_grad[...] += dot((grad_act * silu).astype(jnp.bfloat16), up_ref[...], COLS)

    @pl.when(step == pl.num_programs(0) - 1)
    def _():
        result_ref[:, :latent_width] = sum_out[...].astype(jnp.bfloat16)
        result_ref[:, latent_width:] = sum_grad[...].astype(jnp.bfloat16)


def run_expert(rows, weights):
    count, latent_width = rows.shape[0], rows.shape[1] // 2
    padded = weights.shape[1] // 3
    steps = padded // CHUNK
    halves = latent_width // CHUNK
    out_base = 2 * padded // latent_width
    return pl.pallas_call(
        expert_kernel,
        grid=(steps,),
        in_specs=[
            pl.BlockSpec((count, 2 * latent_width), lambda j: (0, 0)),
            pl.BlockSpec((latent_width, CHUNK), lambda j: (0, j)),
            pl.BlockSpec((latent_width, CHUNK), lambda j: (0, steps + j)),
            pl.BlockSpec((CHUNK, latent_width), lambda j: (j % halves, out_base + j // halves)),
        ],
        out_specs=pl.BlockSpec((count, 2 * latent_width), lambda j: (0, 0)),
        out_shape=jax.ShapeDtypeStruct((count, 2 * latent_width), jnp.bfloat16),
        scratch_shapes=[pltpu.VMEM((count, latent_width), jnp.float32)] * 2,
        compiler_params=LARGE,
        cost_estimate=pl.CostEstimate(
            flops=12 * count * latent_width * padded,
            bytes_accessed=2 * (weights.size + 2 * rows.size),
            transcendentals=count * padded,
        ),
    )(rows, weights, weights, weights)


def swap_kernel(core_ref, tokens_ref, cotangent_ref, down_ref, up_ref, rows_ref, weights_ref, sems):
    other = 1 - core_ref[0]
    features = tokens_ref.shape[3]
    latent_width = down_ref.shape[1]
    copies = [
        pltpu.make_async_copy(
            tokens_ref.at[:, other], rows_ref.at[:, :, pl.ds(0, features)], sems.at[0]
        ),
        pltpu.make_async_copy(
            cotangent_ref.at[:, other], rows_ref.at[:, :, pl.ds(features, features)], sems.at[1]
        ),
    ]
    for copy in copies:
        copy.start()
    weights_ref[:, :latent_width] = down_ref[...]
    weights_ref[:, latent_width:] = up_ref[...].T
    for copy in copies:
        copy.wait()


def swap_operands(core, tokens, cotangent, down_proj, up_proj):
    chips, _, tok_rows, features = tokens.shape
    latent_width = down_proj.shape[1]
    return pl.pallas_call(
        swap_kernel,
        in_specs=[
            pl.BlockSpec(memory_space=pltpu.SMEM),
            pl.BlockSpec(memory_space=pl.ANY),
            pl.BlockSpec(memory_space=pl.ANY),
            pl.BlockSpec(memory_space=pltpu.VMEM),
            pl.BlockSpec(memory_space=pltpu.VMEM),
        ],
        out_specs=[pl.BlockSpec(memory_space=pl.ANY), pl.BlockSpec(memory_space=pltpu.VMEM)],
        out_shape=[
            jax.ShapeDtypeStruct((chips, tok_rows, 2 * features), jnp.bfloat16),
            jax.ShapeDtypeStruct((features, 2 * latent_width), jnp.bfloat16),
        ],
        scratch_shapes=[pltpu.SemaphoreType.DMA((2,))],
        compiler_params=LARGE,
    )(core, tokens, cotangent, down_proj, up_proj)


def latent_kernel(
    core_ref, tokens_ref, cotangent_ref, rows_ref, down_ref, up_ref, weights_ref, latent_ref, grad_ref
):
    features = tokens_ref.shape[3]
    latent_width = down_ref.shape[1]
    count = latent_ref.shape[0]
    down = jnp.concatenate([down_ref[...], weights_ref[:, :latent_width]], axis=0)
    up = jnp.concatenate([up_ref[...].T, weights_ref[:, latent_width:]], axis=0)
    rows = rows_ref[...].reshape(count, 2 * features)
    kept = tokens_ref[...].reshape(count, features)
    left = jnp.concatenate([kept, rows[:, :features]], axis=1)
    latent_ref[...] = dot(left, down).astype(jnp.bfloat16)
    kept = cotangent_ref[...].reshape(count, features)
    left = jnp.concatenate([kept, rows[:, features:]], axis=1)
    grad_ref[...] = dot(left, up).astype(jnp.bfloat16)


def chip_latents(core, tokens, cotangent, rows, down_proj, up_proj, weights):
    chips, _, tok_rows, features = tokens.shape
    latent_width = down_proj.shape[1]
    count = chips * tok_rows
    mine = pl.BlockSpec((chips, 1, tok_rows, features), lambda i, core: (0, core[0], 0, 0))
    whole = lambda array: pl.BlockSpec(array.shape, lambda i, core: (0,) * array.ndim)
    out = jax.ShapeDtypeStruct((count, latent_width), jnp.bfloat16)
    return pl.pallas_call(
        latent_kernel,
        grid_spec=pltpu.PrefetchScalarGridSpec(
            num_scalar_prefetch=1,
            grid=(1,),
            in_specs=[mine, mine, whole(rows), whole(down_proj), whole(up_proj), whole(weights)],
            out_specs=[whole(out)] * 2,
        ),
        out_shape=[out] * 2,
        compiler_params=SMALL,
    )(core, tokens, cotangent, rows, down_proj, up_proj, weights)


def grads_kernel(latents_ref, cotangent_ref, tokens_ref, result_ref, sum_up, sum_down):
    step = pl.program_id(0)
    features = tokens_ref.shape[1]
    latent_width = sum_up.shape[1]

    @pl.when(step == 0)
    def _():
        sum_up[...] = jnp.zeros_like(sum_up)
        sum_down[...] = jnp.zeros_like(sum_down)

    sum_up[...] += dot(cotangent_ref[...], latents_ref[:, :latent_width], ROWS)
    sum_down[...] += dot(tokens_ref[...], latents_ref[:, latent_width:], ROWS)

    @pl.when(step == pl.num_programs(0) - 1)
    def _():
        result_ref[:, :features] = sum_up[...].T.astype(jnp.bfloat16)
        for block in range(latent_width // features):
            here = slice(block * features, (block + 1) * features)
            result_ref[here, features:] = sum_down[:, here].astype(jnp.bfloat16)


def projection_grads(latents, cotangent, tokens):
    count, features = tokens.shape
    latent_width = latents.shape[1] // 2
    rows = count // 4
    return pl.pallas_call(
        grads_kernel,
        grid=(4,),
        in_specs=[
            pl.BlockSpec((rows, 2 * latent_width), lambda i: (i, 0)),
            pl.BlockSpec((rows, features), lambda i: (i, 0)),
            pl.BlockSpec((rows, features), lambda i: (i, 0)),
        ],
        out_specs=pl.BlockSpec((latent_width, 2 * features), lambda i: (0, 0)),
        out_shape=jax.ShapeDtypeStruct((latent_width, 2 * features), jnp.bfloat16),
        scratch_shapes=[pltpu.VMEM((features, latent_width), jnp.float32)] * 2,
        compiler_params=LARGE,
    )(latents, cotangent, tokens)


def unpack_kernel(scale, packed_ref, down_ref, up_ref):
    latent_width, features = up_ref.shape
    up_ref[...] = packed_ref[:, :features].astype(jnp.float32) * scale
    for block in range(latent_width // features):
        here = slice(block * features, (block + 1) * features)
        down_ref[:, here] = packed_ref[here, features:].astype(jnp.float32) * scale


def unpack_grads(packed, scale):
    latent_width, features = packed.shape[0], packed.shape[1] // 2
    return pl.pallas_call(
        functools.partial(unpack_kernel, scale),
        out_shape=[
            jax.ShapeDtypeStruct((features, latent_width), jnp.float32),
            jax.ShapeDtypeStruct((latent_width, features), jnp.float32),
        ],
        compiler_params=SMALL,
    )(packed)


def on_device(tokens, cotangent, down_proj, up_proj, routes, gate_weights, expert_in, expert_out):
    expert = ("z", "c")
    chips = lax.axis_size("z")
    core = lax.axis_index("c")
    groups = chips * CORES
    dp = lax.axis_size("dp")
    tok_rows = routes.shape[0]
    group_rows = tokens.shape[0]
    features = tokens.shape[1]
    latent_width = down_proj.shape[1]
    capacity = min(tok_rows, tok_rows * TOPK * 5 // (4 * groups))
    slot_count = groups * capacity
    grad_scale = 1.0 / math.sqrt(group_rows * dp)
    bf16 = jnp.bfloat16

    swap = [(0, 1), (1, 0)]

    blocked = (chips, CORES, tok_rows, features)
    token_blocks = tokens.reshape(blocked)
    cotangent_blocks = cotangent.reshape(blocked)
    place = core.reshape(1).astype(jnp.int32)
    given = swap_operands(place, token_blocks, cotangent_blocks, down_proj, up_proj)
    got_rows, got_weights = (lax.ppermute(array, "c", swap) for array in given)
    latent, parts = chip_latents(
        place, token_blocks, cotangent_blocks, got_rows, down_proj, up_proj, got_weights
    )
    weights = lax.all_gather(packed_weights(expert_in, expert_out, dp), "dp", axis=0, tiled=True)

    spread, weighted = slot_tables(routes, gate_weights, groups, capacity)
    slot_gate = jnp.sum(weighted, axis=1, keepdims=True)
    gate_high = weighted.astype(bf16)
    gate_low = (weighted - gate_high.astype(jnp.float32)).astype(bf16)

    def exchange(rows):
        return lax.all_to_all(
            rows.reshape(groups, capacity, rows.shape[1]),
            expert,
            split_axis=0,
            concat_axis=0,
            tiled=True,
        ).reshape(slot_count, rows.shape[1])

    latent = lax.psum_scatter(latent, "z", scatter_dimension=0, tiled=True)
    parts = parts.reshape(chips, tok_rows, latent_width)
    parts = lax.all_to_all(parts, "z", split_axis=0, concat_axis=0, tiled=True)
    latent_out_grad = jnp.sum(parts.astype(jnp.float32), axis=0).astype(bf16)
    outgoing = [dot(spread, latent), dot(spread, latent_out_grad) * slot_gate]
    result = run_expert(exchange(jnp.concatenate(outgoing, axis=1).astype(bf16)), weights)
    returned = exchange(result)
    returned_out = returned[:, :latent_width]
    latent_out = (dot(gate_high, returned_out, ROWS) + dot(gate_low, returned_out, ROWS)).astype(
        bf16
    )
    latent_grad = dot(spread, returned[:, latent_width:], ROWS).astype(bf16)

    latents = jnp.concatenate([latent_out, latent_grad], axis=1)
    latents = lax.all_gather(latents, expert, axis=0, tiled=True)
    all_out = latents[:, :latent_width]
    all_grad = latents[:, latent_width:]
    grads = projection_grads(latents, cotangent, tokens)
    grads = grads.reshape(dp, latent_width // dp, 2 * features)
    grads = lax.all_to_all(grads, "dp", split_axis=0, concat_axis=0, tiled=True)
    mixed = dot(all_out, up_proj).astype(bf16)
    input_grad = dot(all_grad, down_proj, COLS).astype(bf16)
    summed = jnp.sum(grads.astype(jnp.float32), axis=0).astype(bf16)
    summed = jnp.broadcast_to(summed[None], grads.shape)
    summed = lax.all_to_all(summed, "dp", split_axis=0, concat_axis=0, tiled=True)
    down_grad, up_grad = unpack_grads(summed.reshape(latent_width, 2 * features), grad_scale)
    return mixed, input_grad, down_grad, up_grad


def solution(mesh):
    dp, experts = mesh.devices.shape
    fine = Mesh(mesh.devices.reshape(dp, experts // CORES, CORES), ("dp", "z", "c"))
    expert = ("z", "c")
    in_specs = (
        P("dp", expert),
        P("dp", expert),
        P(expert, None),
        P(None, expert),
        P(("dp", "z", "c"), None),
        P(("dp", "z", "c"), None),
        P(expert, "dp", None),
        P(expert, "dp", None),
    )
    out_specs = (P("dp", expert), P("dp", expert), P(expert, None), P(None, expert))
    return jax.shard_map(
        on_device, mesh=fine, in_specs=in_specs, out_specs=out_specs, check_vma=False
    )
```

```python
import functools
import math

import jax
import jax.numpy as jnp
from jax import lax
from jax.experimental import pallas as pl
from jax.experimental.pallas import tpu as pltpu
from jax.sharding import Mesh
from jax.sharding import PartitionSpec as P

TOPK = 4
CORES = 2
CHUNK = 256
FIRST = 256
SMALL = pltpu.CompilerParams(vmem_limit_bytes=16 * 1024 * 1024)
LARGE = pltpu.CompilerParams(vmem_limit_bytes=56 * 1024 * 1024)
INNER = (((1,), (0,)), ((), ()))
COLS = (((1,), (1,)), ((), ()))
ROWS = (((0,), (0,)), ((), ()))


def dot(left, right, dims=INNER):
    return lax.dot_general(left, right, dims, preferred_element_type=jnp.float32)


def slot_tables(routes, gate_weights, experts, capacity):
    flat_routes = routes.reshape(-1)
    onehot = (flat_routes[:, None] == jnp.arange(experts, dtype=jnp.int32)[None, :]).astype(
        jnp.int32
    )
    before = jnp.cumsum(onehot, axis=0) - onehot
    position = jnp.sum(before * onehot, axis=1)
    slot = (flat_routes * capacity + position).reshape(routes.shape)
    slot_ids = jnp.arange(experts * capacity, dtype=jnp.int32)
    matches = slot.T[:, None, :] == slot_ids[None, :, None]
    spread = jnp.any(matches, axis=0)
    weighted = jnp.sum(jnp.where(matches, gate_weights.T[:, None, :], 0.0), axis=0)
    return spread.astype(jnp.bfloat16), weighted


def packed_weights(expert_in, expert_out, dp):
    in_rows, width = expert_in.shape[1:]
    own, latent_width = expert_out.shape[1:]
    hidden = width // 2
    tiles = -(-own // in_rows)
    place = jnp.arange(tiles * dp * in_rows, dtype=jnp.int32)
    tile, device, row = place // (dp * in_rows), place // in_rows % dp, place % in_rows
    unit = tile * in_rows + row
    source = jnp.where(unit < own, device * own + unit, -1)
    pick = (jnp.arange(hidden, dtype=jnp.int32)[:, None] == source[None, :]).astype(jnp.bfloat16)
    both = jnp.concatenate([expert_in[0, :, :hidden], expert_in[0, :, hidden:]], axis=0)
    both = dot(both, pick).astype(jnp.bfloat16)
    rows = jnp.pad(expert_out[0], ((0, tiles * in_rows - own), (0, 0)))
    rows = [rows[t * in_rows : (t + 1) * in_rows] for t in range(tiles)]
    return jnp.concatenate([both[:in_rows], both[in_rows:], *rows], axis=1)


def expert_kernel(rows_ref, gate_ref, up_ref, out_ref, result_ref, sum_out, sum_grad):
    step = pl.program_id(0)
    latent_width = sum_out.shape[1]

    @pl.when(step == 0)
    def _():
        sum_out[...] = jnp.zeros_like(sum_out)
        sum_grad[...] = jnp.zeros_like(sum_grad)

    rows = rows_ref[:, :latent_width]
    gate_part = dot(rows, gate_ref[...])
    up_part = dot(rows, up_ref[...])
    grad_act = dot(rows_ref[:, latent_width:], out_ref[...], COLS)
    sigmoid_gate = jax.nn.sigmoid(gate_part)
    silu = gate_part * sigmoid_gate
    sum_out[...] += dot((silu * up_part).astype(jnp.bfloat16), out_ref[...])
    grad_gate = grad_act * up_part * sigmoid_gate * (1.0 + gate_part * (1.0 - sigmoid_gate))
    sum_grad[...] += dot(grad_gate.astype(jnp.bfloat16), gate_ref[...], COLS)
    sum_grad[...] += dot((grad_act * silu).astype(jnp.bfloat16), up_ref[...], COLS)

    @pl.when(step == pl.num_programs(0) - 1)
    def _():
        result_ref[:, :latent_width] = sum_out[...].astype(jnp.bfloat16)
        result_ref[:, latent_width:] = sum_grad[...].astype(jnp.bfloat16)


def run_expert(rows, weights):
    count, latent_width = rows.shape[0], rows.shape[1] // 2
    padded = weights.shape[1] // 3
    steps = padded // CHUNK
    halves = latent_width // CHUNK
    out_base = 2 * padded // latent_width
    return pl.pallas_call(
        expert_kernel,
        grid=(steps,),
        in_specs=[
            pl.BlockSpec((count, 2 * latent_width), lambda j: (0, 0)),
            pl.BlockSpec((latent_width, CHUNK), lambda j: (0, j)),
            pl.BlockSpec((latent_width, CHUNK), lambda j: (0, steps + j)),
            pl.BlockSpec((CHUNK, latent_width), lambda j: (j % halves, out_base + j // halves)),
        ],
        out_specs=pl.BlockSpec((count, 2 * latent_width), lambda j: (0, 0)),
        out_shape=jax.ShapeDtypeStruct((count, 2 * latent_width), jnp.bfloat16),
        scratch_shapes=[pltpu.VMEM((count, latent_width), jnp.float32)] * 2,
        compiler_params=pltpu.CompilerParams(vmem_limit_bytes=32 * 1024 * 1024),
        cost_estimate=pl.CostEstimate(
            flops=12 * count * latent_width * padded,
            bytes_accessed=2 * (weights.size + 2 * rows.size),
            transcendentals=count * padded,
        ),
    )(rows, weights, weights, weights)


def swap_kernel(core_ref, tokens_ref, cotangent_ref, down_ref, up_ref, rows_ref, weights_ref, sems):
    other = 1 - core_ref[0]
    features = tokens_ref.shape[3]
    latent_width = down_ref.shape[1]
    copies = [
        pltpu.make_async_copy(
            tokens_ref.at[:, other], rows_ref.at[:, :, pl.ds(0, features)], sems.at[0]
        ),
        pltpu.make_async_copy(
            cotangent_ref.at[:, other], rows_ref.at[:, :, pl.ds(features, features)], sems.at[1]
        ),
    ]
    for copy in copies:
        copy.start()
    weights_ref[:, :latent_width] = down_ref[...]
    weights_ref[:, latent_width:] = up_ref[...].T
    for copy in copies:
        copy.wait()


def swap_operands(core, tokens, cotangent, down_proj, up_proj):
    chips, _, tok_rows, features = tokens.shape
    latent_width = down_proj.shape[1]
    return pl.pallas_call(
        swap_kernel,
        in_specs=[
            pl.BlockSpec(memory_space=pltpu.SMEM),
            pl.BlockSpec(memory_space=pl.ANY),
            pl.BlockSpec(memory_space=pl.ANY),
            pl.BlockSpec(memory_space=pltpu.VMEM),
            pl.BlockSpec(memory_space=pltpu.VMEM),
        ],
        out_specs=[pl.BlockSpec(memory_space=pltpu.VMEM)] * 2,
        out_shape=[
            jax.ShapeDtypeStruct((chips, tok_rows, 2 * features), jnp.bfloat16),
            jax.ShapeDtypeStruct((features, 2 * latent_width), jnp.bfloat16),
        ],
        scratch_shapes=[pltpu.SemaphoreType.DMA((2,))],
        compiler_params=LARGE,
    )(core, tokens, cotangent, down_proj, up_proj)


def latent_kernel(
    core_ref, tokens_ref, cotangent_ref, rows_ref, down_ref, up_ref, weights_ref, first_ref, rest_ref
):
    features = tokens_ref.shape[3]
    latent_width = down_ref.shape[1]
    count, width = first_ref.shape
    blocks = rest_ref.shape[:2]
    down = jnp.concatenate([down_ref[...], weights_ref[:, :latent_width]], axis=0)
    up = jnp.concatenate([up_ref[...].T, weights_ref[:, latent_width:]], axis=0)
    rows = rows_ref[...].reshape(count, 2 * features)
    kept = tokens_ref[...].reshape(count, features)
    left = jnp.concatenate([kept, rows[:, :features]], axis=1)
    first_ref[...] = dot(left, down[:, :width]).astype(jnp.bfloat16)
    part = dot(left, down[:, width:]).astype(jnp.bfloat16)
    rest_ref[:, :, : latent_width - width] = part.reshape(*blocks, latent_width - width)
    kept = cotangent_ref[...].reshape(count, features)
    left = jnp.concatenate([kept, rows[:, features:]], axis=1)
    part = dot(left, up).astype(jnp.bfloat16)
    rest_ref[:, :, latent_width - width :] = part.reshape(*blocks, latent_width)


def chip_latents(core, tokens, cotangent, rows, down_proj, up_proj, weights):
    chips, _, tok_rows, features = tokens.shape
    latent_width = down_proj.shape[1]
    count = chips * tok_rows
    mine = pl.BlockSpec((chips, 1, tok_rows, features), lambda i, core: (0, core[0], 0, 0))
    whole = lambda array: pl.BlockSpec(array.shape, lambda i, core: (0,) * array.ndim)
    out = [
        jax.ShapeDtypeStruct((count, FIRST), jnp.bfloat16),
        jax.ShapeDtypeStruct((chips, tok_rows, 2 * latent_width - FIRST), jnp.bfloat16),
    ]
    return pl.pallas_call(
        latent_kernel,
        grid_spec=pltpu.PrefetchScalarGridSpec(
            num_scalar_prefetch=1,
            grid=(1,),
            in_specs=[mine, mine, whole(rows), whole(down_proj), whole(up_proj), whole(weights)],
            out_specs=[whole(array) for array in out],
        ),
        out_shape=out,
        compiler_params=SMALL,
    )(core, tokens, cotangent, rows, down_proj, up_proj, weights)


def dispatch_kernel(first_ref, parts_ref, spread_ref, gate_ref, result_ref):
    width = first_ref.shape[1]
    latent_width = result_ref.shape[1] // 2
    rest = parts_ref[0].astype(jnp.float32)
    for chip in range(1, parts_ref.shape[0]):
        rest += parts_ref[chip].astype(jnp.float32)
    rest = rest.astype(jnp.bfloat16)
    spread = spread_ref[...]
    result_ref[:, :width] = dot(spread, first_ref[...]).astype(jnp.bfloat16)
    placed = dot(spread, rest[:, : latent_width - width])
    result_ref[:, width:latent_width] = placed.astype(jnp.bfloat16)
    placed = dot(spread, rest[:, latent_width - width :]) * gate_ref[...]
    result_ref[:, latent_width:] = placed.astype(jnp.bfloat16)


def dispatched_rows(first, parts, spread, slot_gate):
    columns = first.shape[1] + parts.shape[2]
    return pl.pallas_call(
        dispatch_kernel,
        out_shape=jax.ShapeDtypeStruct((spread.shape[0], columns), jnp.bfloat16),
        compiler_params=SMALL,
    )(first, parts, spread, slot_gate)


def unpack_kernel(scale, packed_ref, down_ref, up_ref):
    features = up_ref.shape[1]
    up_ref[...] = packed_ref[:, :features].astype(jnp.float32) * scale
    down_ref[...] = packed_ref[:, features:].astype(jnp.float32).T * scale


def unpack_grads(packed, scale):
    latent_width, features = packed.shape[0], packed.shape[1] // 2
    return pl.pallas_call(
        functools.partial(unpack_kernel, scale),
        out_shape=[
            jax.ShapeDtypeStruct((features, latent_width), jnp.float32),
            jax.ShapeDtypeStruct((latent_width, features), jnp.float32),
        ],
        compiler_params=SMALL,
    )(packed)


def on_device(tokens, cotangent, down_proj, up_proj, routes, gate_weights, expert_in, expert_out):
    expert = ("z", "c")
    chips = lax.axis_size("z")
    core = lax.axis_index("c")
    groups = chips * CORES
    dp = lax.axis_size("dp")
    tok_rows = routes.shape[0]
    group_rows = tokens.shape[0]
    features = tokens.shape[1]
    latent_width = down_proj.shape[1]
    capacity = min(tok_rows, tok_rows * TOPK * 5 // (4 * groups))
    slot_count = groups * capacity
    grad_scale = 1.0 / math.sqrt(group_rows * dp)
    bf16 = jnp.bfloat16

    swap = [(0, 1), (1, 0)]

    blocked = (chips, CORES, tok_rows, features)
    token_blocks = tokens.reshape(blocked)
    cotangent_blocks = cotangent.reshape(blocked)
    place = core.reshape(1).astype(jnp.int32)
    given = swap_operands(place, token_blocks, cotangent_blocks, down_proj, up_proj)
    got_rows, got_weights = (lax.ppermute(array, "c", swap) for array in given)
    packed, got_rows = lax.optimization_barrier(
        (packed_weights(expert_in, expert_out, dp), got_rows)
    )
    weights = lax.all_gather(packed, "dp", axis=0, tiled=True)
    first, parts = chip_latents(
        place, token_blocks, cotangent_blocks, got_rows, down_proj, up_proj, got_weights
    )
    first = lax.psum_scatter(first, "z", scatter_dimension=0, tiled=True)
    parts = lax.all_to_all(parts, "z", split_axis=0, concat_axis=0, tiled=True)

    spread, weighted = slot_tables(routes, gate_weights, groups, capacity)
    slot_gate = jnp.sum(weighted, axis=1, keepdims=True)
    gate_high = weighted.astype(bf16)
    gate_low = (weighted - gate_high.astype(jnp.float32)).astype(bf16)

    def exchange(rows):
        return lax.all_to_all(
            rows.reshape(groups, capacity, rows.shape[1]),
            expert,
            split_axis=0,
            concat_axis=0,
            tiled=True,
        ).reshape(slot_count, rows.shape[1])

    outgoing = dispatched_rows(first, parts, spread, slot_gate)
    result = run_expert(exchange(outgoing), weights)
    returned = exchange(result)
    returned_out = returned[:, :latent_width]
    latent_out = (dot(gate_high, returned_out, ROWS) + dot(gate_low, returned_out, ROWS)).astype(
        bf16
    )
    latent_grad = dot(spread, returned[:, latent_width:], ROWS).astype(bf16)

    latents = jnp.concatenate([latent_out, latent_grad], axis=1)
    latents = lax.all_gather(latents, expert, axis=0, tiled=True)
    all_out = latents[:, :latent_width]
    all_grad = latents[:, latent_width:]
    up_part_grad = dot(all_out, cotangent, ROWS)
    down_part_grad = dot(all_grad, tokens, ROWS)
    grads = jnp.concatenate([up_part_grad, down_part_grad], axis=1).astype(bf16)
    grads = grads.reshape(dp, latent_width // dp, 2 * features)
    grads = lax.all_to_all(grads, "dp", split_axis=0, concat_axis=0, tiled=True)
    mixed = dot(all_out, up_proj).astype(bf16)
    input_grad = dot(all_grad, down_proj, COLS).astype(bf16)
    summed = jnp.sum(grads.astype(jnp.float32), axis=0).astype(bf16)
    summed = jnp.broadcast_to(summed[None], grads.shape)
    summed = lax.all_to_all(summed, "dp", split_axis=0, concat_axis=0, tiled=True)
    down_grad, up_grad = unpack_grads(summed.reshape(latent_width, 2 * features), grad_scale)
    return mixed, input_grad, down_grad, up_grad


def solution(mesh):
    dp, experts = mesh.devices.shape
    fine = Mesh(mesh.devices.reshape(dp, experts // CORES, CORES), ("dp", "z", "c"))
    expert = ("z", "c")
    in_specs = (
        P("dp", expert),
        P("dp", expert),
        P(expert, None),
        P(None, expert),
        P(("dp", "z", "c"), None),
        P(("dp", "z", "c"), None),
        P(expert, "dp", None),
        P(expert, "dp", None),
    )
    out_specs = (P("dp", expert), P("dp", expert), P(expert, None), P(None, expert))
    return jax.shard_map(
        on_device, mesh=fine, in_specs=in_specs, out_specs=out_specs, check_vma=False
    )
```

```python
import functools
import math

import jax
import jax.numpy as jnp
from jax import lax
from jax.experimental import pallas as pl
from jax.experimental.pallas import tpu as pltpu
from jax.sharding import Mesh
from jax.sharding import PartitionSpec as P

TOPK = 4
CORES = 2
CHUNK = 256
ACROSS = 4
SMALL = pltpu.CompilerParams(vmem_limit_bytes=16 * 1024 * 1024)
LARGE = pltpu.CompilerParams(vmem_limit_bytes=56 * 1024 * 1024)
INNER = (((1,), (0,)), ((), ()))
COLS = (((1,), (1,)), ((), ()))
ROWS = (((0,), (0,)), ((), ()))


def dot(left, right, dims=INNER):
    return lax.dot_general(left, right, dims, preferred_element_type=jnp.float32)


def slot_tables(routes, gate_weights, experts, capacity):
    flat_routes = routes.reshape(-1)
    onehot = (flat_routes[:, None] == jnp.arange(experts, dtype=jnp.int32)[None, :]).astype(
        jnp.int32
    )
    before = jnp.cumsum(onehot, axis=0) - onehot
    position = jnp.sum(before * onehot, axis=1)
    slot = (flat_routes * capacity + position).reshape(routes.shape)
    slot_ids = jnp.arange(experts * capacity, dtype=jnp.int32)
    matches = slot.T[:, None, :] == slot_ids[None, :, None]
    spread = jnp.any(matches, axis=0)
    weighted = jnp.sum(jnp.where(matches, gate_weights.T[:, None, :], 0.0), axis=0)
    return spread.astype(jnp.bfloat16), weighted


def packed_weights(expert_in, expert_out, dp):
    in_rows, width = expert_in.shape[1:]
    own, latent_width = expert_out.shape[1:]
    hidden = width // 2
    tiles = -(-own // in_rows)
    place = jnp.arange(tiles * dp * in_rows, dtype=jnp.int32)
    tile, device, row = place // (dp * in_rows), place // in_rows % dp, place % in_rows
    unit = tile * in_rows + row
    source = jnp.where(unit < own, device * own + unit, -1)
    pick = (jnp.arange(hidden, dtype=jnp.int32)[:, None] == source[None, :]).astype(jnp.bfloat16)
    both = jnp.concatenate([expert_in[0, :, :hidden], expert_in[0, :, hidden:]], axis=0)
    both = dot(both, pick).astype(jnp.bfloat16)
    rows = jnp.pad(expert_out[0], ((0, tiles * in_rows - own), (0, 0)))
    rows = [rows[t * in_rows : (t + 1) * in_rows] for t in range(tiles)]
    return jnp.concatenate([both[:in_rows], both[in_rows:], *rows], axis=1)


def expert_kernel(rows_ref, gate_ref, up_ref, out_ref, result_ref, sum_out, sum_grad):
    step = pl.program_id(0)
    latent_width = sum_out.shape[1]

    @pl.when(step == 0)
    def _():
        sum_out[...] = jnp.zeros_like(sum_out)
        sum_grad[...] = jnp.zeros_like(sum_grad)

    rows = rows_ref[:, :latent_width]
    gate_part = dot(rows, gate_ref[...])
    up_part = dot(rows, up_ref[...])
    grad_act = dot(rows_ref[:, latent_width:], out_ref[...], COLS)
    sigmoid_gate = jax.nn.sigmoid(gate_part)
    silu = gate_part * sigmoid_gate
    sum_out[...] += dot((silu * up_part).astype(jnp.bfloat16), out_ref[...])
    grad_gate = grad_act * up_part * sigmoid_gate * (1.0 + gate_part * (1.0 - sigmoid_gate))
    sum_grad[...] += dot(grad_gate.astype(jnp.bfloat16), gate_ref[...], COLS)
    sum_grad[...] += dot((grad_act * silu).astype(jnp.bfloat16), up_ref[...], COLS)

    @pl.when(step == pl.num_programs(0) - 1)
    def _():
        result_ref[:, :latent_width] = sum_out[...].astype(jnp.bfloat16)
        result_ref[:, latent_width:] = sum_grad[...].astype(jnp.bfloat16)


def run_expert(rows, weights):
    count, latent_width = rows.shape[0], rows.shape[1] // 2
    padded = weights.shape[1] // 3
    steps = padded // CHUNK
    halves = latent_width // CHUNK
    out_base = 2 * padded // latent_width
    return pl.pallas_call(
        expert_kernel,
        grid=(steps,),
        in_specs=[
            pl.BlockSpec((count, 2 * latent_width), lambda j: (0, 0)),
            pl.BlockSpec((latent_width, CHUNK), lambda j: (0, j)),
            pl.BlockSpec((latent_width, CHUNK), lambda j: (0, steps + j)),
            pl.BlockSpec((CHUNK, latent_width), lambda j: (j % halves, out_base + j // halves)),
        ],
        out_specs=pl.BlockSpec((count, 2 * latent_width), lambda j: (0, 0)),
        out_shape=jax.ShapeDtypeStruct((count, 2 * latent_width), jnp.bfloat16),
        scratch_shapes=[pltpu.VMEM((count, latent_width), jnp.float32)] * 2,
        compiler_params=pltpu.CompilerParams(vmem_limit_bytes=50 * 1024 * 1024),
        cost_estimate=pl.CostEstimate(
            flops=12 * count * latent_width * padded,
            bytes_accessed=2 * (weights.size + 2 * rows.size),
            transcendentals=count * padded,
        ),
    )(rows, weights, weights, weights)


def swap_kernel(core_ref, tokens_ref, cotangent_ref, down_ref, up_ref, rows_ref, weights_ref, sems):
    other = 1 - core_ref[0]
    features = tokens_ref.shape[3]
    latent_width = down_ref.shape[1]
    copies = [
        pltpu.make_async_copy(
            tokens_ref.at[:, other], rows_ref.at[:, :, pl.ds(0, features)], sems.at[0]
        ),
        pltpu.make_async_copy(
            cotangent_ref.at[:, other], rows_ref.at[:, :, pl.ds(features, features)], sems.at[1]
        ),
    ]
    for copy in copies:
        copy.start()
    weights_ref[:, :latent_width] = down_ref[...]
    weights_ref[:, latent_width:] = up_ref[...].T
    for copy in copies:
        copy.wait()


def swap_operands(core, tokens, cotangent, down_proj, up_proj):
    chips, _, tok_rows, features = tokens.shape
    latent_width = down_proj.shape[1]
    return pl.pallas_call(
        swap_kernel,
        in_specs=[
            pl.BlockSpec(memory_space=pltpu.SMEM),
            pl.BlockSpec(memory_space=pl.ANY),
            pl.BlockSpec(memory_space=pl.ANY),
            pl.BlockSpec(memory_space=pltpu.VMEM),
            pl.BlockSpec(memory_space=pltpu.VMEM),
        ],
        out_specs=[pl.BlockSpec(memory_space=pltpu.VMEM)] * 2,
        out_shape=[
            jax.ShapeDtypeStruct((chips, tok_rows, 2 * features), jnp.bfloat16),
            jax.ShapeDtypeStruct((features, 2 * latent_width), jnp.bfloat16),
        ],
        scratch_shapes=[pltpu.SemaphoreType.DMA((2,))],
        compiler_params=LARGE,
    )(core, tokens, cotangent, down_proj, up_proj)


def latent_kernel(
    core_ref, tokens_ref, cotangent_ref, rows_ref, down_ref, up_ref, weights_ref, result_ref
):
    features = tokens_ref.shape[3]
    latent_width = down_ref.shape[1]
    count = result_ref.shape[0]
    down = jnp.concatenate([down_ref[...], weights_ref[:, :latent_width]], axis=0)
    up = jnp.concatenate([up_ref[...].T, weights_ref[:, latent_width:]], axis=0)
    rows = rows_ref[...].reshape(count, 2 * features)
    kept = tokens_ref[...].reshape(count, features)
    left = jnp.concatenate([kept, rows[:, :features]], axis=1)
    result_ref[:, :latent_width] = dot(left, down).astype(jnp.bfloat16)
    kept = cotangent_ref[...].reshape(count, features)
    left = jnp.concatenate([kept, rows[:, features:]], axis=1)
    result_ref[:, latent_width:] = dot(left, up).astype(jnp.bfloat16)


def chip_latents(core, tokens, cotangent, rows, down_proj, up_proj, weights):
    chips, _, tok_rows, features = tokens.shape
    latent_width = down_proj.shape[1]
    count = chips * tok_rows
    mine = pl.BlockSpec((chips, 1, tok_rows, features), lambda i, core: (0, core[0], 0, 0))
    whole = lambda array: pl.BlockSpec(array.shape, lambda i, core: (0,) * array.ndim)
    out = jax.ShapeDtypeStruct((count, 2 * latent_width), jnp.bfloat16)
    return pl.pallas_call(
        latent_kernel,
        grid_spec=pltpu.PrefetchScalarGridSpec(
            num_scalar_prefetch=1,
            grid=(1,),
            in_specs=[mine, mine, whole(rows), whole(down_proj), whole(up_proj), whole(weights)],
            out_specs=whole(out),
        ),
        out_shape=out,
        compiler_params=SMALL,
    )(core, tokens, cotangent, rows, down_proj, up_proj, weights)


def dispatch_kernel(latents_ref, spread_ref, gate_ref, result_ref):
    latent_width = latents_ref.shape[1] // 2
    placed = dot(spread_ref[...], latents_ref[...])
    result_ref[:, :latent_width] = placed[:, :latent_width].astype(jnp.bfloat16)
    result_ref[:, latent_width:] = (placed[:, latent_width:] * gate_ref[...]).astype(jnp.bfloat16)


def dispatched_rows(latents, spread, slot_gate):
    return pl.pallas_call(
        dispatch_kernel,
        out_shape=jax.ShapeDtypeStruct((spread.shape[0], latents.shape[1]), jnp.bfloat16),
        compiler_params=SMALL,
    )(latents, spread, slot_gate)


def arrange_kernel(place_ref, *refs):
    *parts, result_ref = refs
    for step, part in enumerate(parts):
        result_ref[lax.rem(place_ref[0] + step, len(parts))] = part[...]


def arranged(place, parts):
    out = jax.ShapeDtypeStruct((len(parts), *parts[0].shape), parts[0].dtype)
    return pl.pallas_call(
        arrange_kernel,
        in_specs=[pl.BlockSpec(memory_space=pltpu.SMEM)]
        + [pl.BlockSpec(memory_space=pltpu.VMEM)] * len(parts),
        out_shape=out,
        compiler_params=SMALL,
    )(place, *parts).reshape(-1, parts[0].shape[1])


def unpack_kernel(scale, packed_ref, down_ref, up_ref):
    features = up_ref.shape[1]
    up_ref[...] = packed_ref[:, :features].astype(jnp.float32) * scale
    down_ref[...] = packed_ref[:, features:].astype(jnp.float32).T * scale


def unpack_grads(packed, scale):
    latent_width, features = packed.shape[0], packed.shape[1] // 2
    return pl.pallas_call(
        functools.partial(unpack_kernel, scale),
        out_shape=[
            jax.ShapeDtypeStruct((features, latent_width), jnp.float32),
            jax.ShapeDtypeStruct((latent_width, features), jnp.float32),
        ],
        compiler_params=SMALL,
    )(packed)


def on_device(tokens, cotangent, down_proj, up_proj, routes, gate_weights, expert_in, expert_out):
    expert = ("z", "c")
    chips = lax.axis_size("z")
    core = lax.axis_index("c")
    groups = chips * CORES
    dp_axes = ("y", "x")
    dp = lax.axis_size(dp_axes)
    tok_rows = routes.shape[0]
    group_rows = tokens.shape[0]
    features = tokens.shape[1]
    latent_width = down_proj.shape[1]
    capacity = min(tok_rows, tok_rows * TOPK * 5 // (4 * groups))
    slot_count = groups * capacity
    grad_scale = 1.0 / math.sqrt(group_rows * dp)
    bf16 = jnp.bfloat16

    swap = [(0, 1), (1, 0)]

    blocked = (chips, CORES, tok_rows, features)
    token_blocks = tokens.reshape(blocked)
    cotangent_blocks = cotangent.reshape(blocked)
    place = core.reshape(1).astype(jnp.int32)
    given = swap_operands(place, token_blocks, cotangent_blocks, down_proj, up_proj)
    got_rows, got_weights = (lax.ppermute(array, "c", swap) for array in given)
    parts = chip_latents(
        place, token_blocks, cotangent_blocks, got_rows, down_proj, up_proj, got_weights
    )
    latents = lax.psum_scatter(parts, "z", scatter_dimension=0, tiled=True)

    packed = packed_weights(expert_in, expert_out, dp)
    across = lax.axis_size("x")
    neighbours = [packed]
    for step in range(1, across):
        backward = [(i, (i - step) % across) for i in range(across)]
        neighbours.append(lax.ppermute(packed, "x", backward))
    column = lax.axis_index("x").reshape(1).astype(jnp.int32)
    weights = lax.all_gather(arranged(column, neighbours), "y", axis=0, tiled=True)

    spread, weighted = slot_tables(routes, gate_weights, groups, capacity)
    slot_gate = jnp.sum(weighted, axis=1, keepdims=True)
    gate_high = weighted.astype(bf16)
    gate_low = (weighted - gate_high.astype(jnp.float32)).astype(bf16)

    def exchange(rows):
        return lax.all_to_all(
            rows.reshape(groups, capacity, rows.shape[1]),
            expert,
            split_axis=0,
            concat_axis=0,
            tiled=True,
        ).reshape(slot_count, rows.shape[1])

    outgoing = dispatched_rows(latents, spread, slot_gate)
    result = run_expert(exchange(outgoing), weights)
    returned = exchange(result)
    returned_out = returned[:, :latent_width]
    latent_out = (dot(gate_high, returned_out, ROWS) + dot(gate_low, returned_out, ROWS)).astype(
        bf16
    )
    latent_grad = dot(spread, returned[:, latent_width:], ROWS).astype(bf16)

    latents = jnp.concatenate([latent_out, latent_grad], axis=1)
    latents = lax.all_gather(latents, expert, axis=0, tiled=True)
    all_out = latents[:, :latent_width]
    all_grad = latents[:, latent_width:]
    up_part_grad = dot(all_out, cotangent, ROWS)
    down_part_grad = dot(all_grad, tokens, ROWS)
    grads = jnp.concatenate([up_part_grad, down_part_grad], axis=1).astype(bf16)
    grads = grads.reshape(dp, latent_width // dp, 2 * features)
    grads = lax.all_to_all(grads, dp_axes, split_axis=0, concat_axis=0, tiled=True)
    mixed = dot(all_out, up_proj).astype(bf16)
    input_grad = dot(all_grad, down_proj, COLS).astype(bf16)
    summed = jnp.sum(grads.astype(jnp.float32), axis=0).astype(bf16)
    summed = jnp.broadcast_to(summed[None], grads.shape)
    summed = lax.all_to_all(summed, dp_axes, split_axis=0, concat_axis=0, tiled=True)
    down_grad, up_grad = unpack_grads(summed.reshape(latent_width, 2 * features), grad_scale)
    return mixed, input_grad, down_grad, up_grad


def solution(mesh):
    dp, experts = mesh.devices.shape
    across = math.gcd(dp, ACROSS)
    shape = (dp // across, across, experts // CORES, CORES)
    fine = Mesh(mesh.devices.reshape(shape), ("y", "x", "z", "c"))
    group = ("y", "x")
    expert = ("z", "c")
    in_specs = (
        P(group, expert),
        P(group, expert),
        P(expert, None),
        P(None, expert),
        P(("y", "x", "z", "c"), None),
        P(("y", "x", "z", "c"), None),
        P(expert, group, None),
        P(expert, group, None),
    )
    out_specs = (P(group, expert), P(group, expert), P(expert, None), P(None, expert))
    return jax.shard_map(
        on_device, mesh=fine, in_specs=in_specs, out_specs=out_specs, check_vma=False
    )
```

```python
import functools
import math

import jax
import jax.numpy as jnp
from jax import lax
from jax.experimental import pallas as pl
from jax.experimental.pallas import tpu as pltpu
from jax.sharding import Mesh
from jax.sharding import PartitionSpec as P

TOPK = 4
CORES = 2
CHUNK = 256
ACROSS = 4
SMALL = pltpu.CompilerParams(vmem_limit_bytes=16 * 1024 * 1024)
INNER = (((1,), (0,)), ((), ()))
COLS = (((1,), (1,)), ((), ()))
ROWS = (((0,), (0,)), ((), ()))


def dot(left, right, dims=INNER):
    return lax.dot_general(left, right, dims, preferred_element_type=jnp.float32)


def slot_tables(routes, gate_weights, experts, capacity):
    flat_routes = routes.reshape(-1)
    onehot = (flat_routes[:, None] == jnp.arange(experts, dtype=jnp.int32)[None, :]).astype(
        jnp.int32
    )
    before = jnp.cumsum(onehot, axis=0) - onehot
    position = jnp.sum(before * onehot, axis=1)
    slot = (flat_routes * capacity + position).reshape(routes.shape)
    slot_ids = jnp.arange(experts * capacity, dtype=jnp.int32)
    matches = slot.T[:, None, :] == slot_ids[None, :, None]
    to_slot = jnp.any(matches, axis=0).astype(jnp.bfloat16)
    weighted = jnp.sum(jnp.where(matches, gate_weights.T[:, None, :], 0.0), axis=0)
    slot_gate = jnp.sum(weighted, axis=1, keepdims=True)
    matches = slot[:, :, None] == slot_ids[None, None, :]
    to_token = jnp.any(matches, axis=1).astype(jnp.bfloat16)
    weighted = jnp.sum(jnp.where(matches, gate_weights[:, :, None], 0.0), axis=1)
    gate_high = weighted.astype(jnp.bfloat16)
    gate_low = (weighted - gate_high.astype(jnp.float32)).astype(jnp.bfloat16)
    return to_slot, slot_gate, to_token, jnp.concatenate([gate_high, gate_low], axis=0)


def packed_weights(expert_in, expert_out, dp):
    in_rows, width = expert_in.shape[1:]
    own, latent_width = expert_out.shape[1:]
    hidden = width // 2
    tiles = -(-own // in_rows)
    place = jnp.arange(tiles * dp * in_rows, dtype=jnp.int32)
    tile, device, row = place // (dp * in_rows), place // in_rows % dp, place % in_rows
    unit = tile * in_rows + row
    source = jnp.where(unit < own, device * own + unit, -1)
    pick = (jnp.arange(hidden, dtype=jnp.int32)[:, None] == source[None, :]).astype(jnp.bfloat16)
    both = jnp.concatenate([expert_in[0, :, :hidden], expert_in[0, :, hidden:]], axis=0)
    both = dot(both, pick).astype(jnp.bfloat16)
    rows = jnp.pad(expert_out[0], ((0, tiles * in_rows - own), (0, 0)))
    rows = [rows[t * in_rows : (t + 1) * in_rows] for t in range(tiles)]
    return jnp.concatenate([both[:in_rows], both[in_rows:], *rows], axis=1)


def expert_kernel(rows_ref, gate_ref, up_ref, out_ref, result_ref, sum_out, sum_grad):
    step = pl.program_id(0)
    latent_width = sum_out.shape[1]

    @pl.when(step == 0)
    def _():
        sum_out[...] = jnp.zeros_like(sum_out)
        sum_grad[...] = jnp.zeros_like(sum_grad)

    rows = rows_ref[:, :latent_width]
    gate_part = dot(rows, gate_ref[...])
    up_part = dot(rows, up_ref[...])
    grad_act = dot(rows_ref[:, latent_width:], out_ref[...], COLS)
    sigmoid_gate = jax.nn.sigmoid(gate_part)
    silu = gate_part * sigmoid_gate
    sum_out[...] += dot((silu * up_part).astype(jnp.bfloat16), out_ref[...])
    grad_gate = grad_act * up_part * sigmoid_gate * (1.0 + gate_part * (1.0 - sigmoid_gate))
    sum_grad[...] += dot(grad_gate.astype(jnp.bfloat16), gate_ref[...], COLS)
    sum_grad[...] += dot((grad_act * silu).astype(jnp.bfloat16), up_ref[...], COLS)

    @pl.when(step == pl.num_programs(0) - 1)
    def _():
        result_ref[:, :latent_width] = sum_out[...].astype(jnp.bfloat16)
        result_ref[:, latent_width:] = sum_grad[...].astype(jnp.bfloat16)


def run_expert(rows, weights):
    count, latent_width = rows.shape[0], rows.shape[1] // 2
    padded = weights.shape[1] // 3
    steps = padded // CHUNK
    halves = latent_width // CHUNK
    out_base = 2 * padded // latent_width
    return pl.pallas_call(
        expert_kernel,
        grid=(steps,),
        in_specs=[
            pl.BlockSpec((count, 2 * latent_width), lambda j: (0, 0)),
            pl.BlockSpec((latent_width, CHUNK), lambda j: (0, j)),
            pl.BlockSpec((latent_width, CHUNK), lambda j: (0, steps + j)),
            pl.BlockSpec((CHUNK, latent_width), lambda j: (j % halves, out_base + j // halves)),
        ],
        out_specs=pl.BlockSpec((count, 2 * latent_width), lambda j: (0, 0)),
        out_shape=jax.ShapeDtypeStruct((count, 2 * latent_width), jnp.bfloat16),
        scratch_shapes=[pltpu.VMEM((count, latent_width), jnp.float32)] * 2,
        compiler_params=pltpu.CompilerParams(vmem_limit_bytes=50 * 1024 * 1024),
        cost_estimate=pl.CostEstimate(
            flops=12 * count * latent_width * padded,
            bytes_accessed=2 * (weights.size + 2 * rows.size),
            transcendentals=count * padded,
        ),
    )(rows, weights, weights, weights)


def swap_kernel(
    core_ref, tokens_ref, cotangent_ref, down_ref, up_ref, rows_ref, kept_ref, weights_ref, up_here, sems
):
    mine = core_ref[0]
    features = tokens_ref.shape[3]
    latent_width = down_ref.shape[1]
    first, second = pl.ds(0, features), pl.ds(features, features)
    moves = [
        (up_ref, up_here),
        (tokens_ref.at[:, 1 - mine], rows_ref.at[:, :, first]),
        (cotangent_ref.at[:, 1 - mine], rows_ref.at[:, :, second]),
        (down_ref, weights_ref.at[:, pl.ds(0, latent_width)]),
        (tokens_ref.at[:, mine], kept_ref.at[:, :, first]),
        (cotangent_ref.at[:, mine], kept_ref.at[:, :, second]),
    ]
    copies = [pltpu.make_async_copy(*move, sems.at[i]) for i, move in enumerate(moves)]
    for copy in copies:
        copy.start()
    copies[0].wait()
    weights_ref[:, latent_width:] = up_here[...].T
    for copy in copies[1:]:
        copy.wait()


def swap_operands(core, tokens, cotangent, down_proj, up_proj):
    chips, _, tok_rows, features = tokens.shape
    latent_width = down_proj.shape[1]
    rows = jax.ShapeDtypeStruct((chips, tok_rows, 2 * features), jnp.bfloat16)
    return pl.pallas_call(
        swap_kernel,
        in_specs=[pl.BlockSpec(memory_space=pltpu.SMEM)]
        + [pl.BlockSpec(memory_space=pltpu.HBM)] * 4,
        out_specs=[pl.BlockSpec(memory_space=pltpu.VMEM)] * 3,
        out_shape=[rows, rows, jax.ShapeDtypeStruct((features, 2 * latent_width), jnp.bfloat16)],
        scratch_shapes=[
            pltpu.VMEM((latent_width, features), jnp.bfloat16),
            pltpu.SemaphoreType.DMA((6,)),
        ],
        compiler_params=SMALL,
    )(core, tokens, cotangent, down_proj, up_proj)


def latent_kernel(kept_ref, got_ref, here_ref, there_ref, result_ref):
    count = result_ref.shape[0]
    latent_width = here_ref.shape[1] // 2
    features = kept_ref.shape[2] // 2
    kept = kept_ref[...].reshape(count, 2 * features)
    got = got_ref[...].reshape(count, 2 * features)
    for half in range(2):
        rows = slice(half * features, (half + 1) * features)
        here = slice(half * latent_width, (half + 1) * latent_width)
        left = jnp.concatenate([kept[:, rows], got[:, rows]], axis=1)
        right = jnp.concatenate([here_ref[:, here], there_ref[:, here]], axis=0)
        result_ref[:, here] = dot(left, right).astype(jnp.bfloat16)


def chip_latents(kept, got, here, there):
    count = kept.shape[0] * kept.shape[1]
    return pl.pallas_call(
        latent_kernel,
        out_shape=jax.ShapeDtypeStruct((count, here.shape[1]), jnp.bfloat16),
        compiler_params=SMALL,
    )(kept, got, here, there)


def combine_kernel(returned_ref, gates_ref, spread_ref, result_ref):
    latent_width = returned_ref.shape[1] // 2
    count = spread_ref.shape[0]
    gated = dot(gates_ref[...], returned_ref[:, :latent_width])
    result_ref[:, :latent_width] = (gated[:count] + gated[count:]).astype(jnp.bfloat16)
    result_ref[:, latent_width:] = dot(spread_ref[...], returned_ref[:, latent_width:]).astype(
        jnp.bfloat16
    )


def combined_latents(returned, gates, spread):
    return pl.pallas_call(
        combine_kernel,
        out_shape=jax.ShapeDtypeStruct((spread.shape[0], returned.shape[1]), jnp.bfloat16),
        compiler_params=SMALL,
    )(returned, gates, spread)


def share_kernel(pieces_ref, result_ref):
    summed = jnp.sum(pieces_ref[...].astype(jnp.float32), axis=0).astype(jnp.bfloat16)
    result_ref[...] = jnp.broadcast_to(summed[None], result_ref.shape)


def shared_sums(pieces):
    return pl.pallas_call(
        share_kernel,
        out_shape=jax.ShapeDtypeStruct(pieces.shape, jnp.bfloat16),
        compiler_params=SMALL,
    )(pieces)


def dispatch_kernel(latents_ref, spread_ref, gate_ref, result_ref):
    latent_width = latents_ref.shape[1] // 2
    placed = dot(spread_ref[...], latents_ref[...])
    result_ref[:, :latent_width] = placed[:, :latent_width].astype(jnp.bfloat16)
    result_ref[:, latent_width:] = (placed[:, latent_width:] * gate_ref[...]).astype(jnp.bfloat16)


def dispatched_rows(latents, spread, slot_gate):
    return pl.pallas_call(
        dispatch_kernel,
        out_shape=jax.ShapeDtypeStruct((spread.shape[0], latents.shape[1]), jnp.bfloat16),
        compiler_params=SMALL,
    )(latents, spread, slot_gate)


def arrange_kernel(place_ref, *refs):
    *parts, result_ref = refs
    for step, part in enumerate(parts):
        result_ref[lax.rem(place_ref[0] + step, len(parts))] = part[...]


def arranged(place, parts):
    out = jax.ShapeDtypeStruct((len(parts), *parts[0].shape), parts[0].dtype)
    return pl.pallas_call(
        arrange_kernel,
        in_specs=[pl.BlockSpec(memory_space=pltpu.SMEM)]
        + [pl.BlockSpec(memory_space=pltpu.VMEM)] * len(parts),
        out_shape=out,
        compiler_params=SMALL,
    )(place, *parts).reshape(-1, parts[0].shape[1])


def unpack_kernel(scale, packed_ref, down_ref, up_ref):
    features = up_ref.shape[1]
    up_ref[...] = packed_ref[:, :features].astype(jnp.float32) * scale
    down_ref[...] = packed_ref[:, features:].astype(jnp.float32).T * scale


def unpack_grads(packed, scale):
    latent_width, features = packed.shape[0], packed.shape[1] // 2
    return pl.pallas_call(
        functools.partial(unpack_kernel, scale),
        out_shape=[
            jax.ShapeDtypeStruct((features, latent_width), jnp.float32),
            jax.ShapeDtypeStruct((latent_width, features), jnp.float32),
        ],
        compiler_params=SMALL,
    )(packed)


def on_device(tokens, cotangent, down_proj, up_proj, routes, gate_weights, expert_in, expert_out):
    expert = ("z", "c")
    chips = lax.axis_size("z")
    core = lax.axis_index("c")
    groups = chips * CORES
    dp_axes = ("y", "x")
    dp = lax.axis_size(dp_axes)
    tok_rows = routes.shape[0]
    group_rows = tokens.shape[0]
    features = tokens.shape[1]
    latent_width = down_proj.shape[1]
    capacity = min(tok_rows, tok_rows * TOPK * 5 // (4 * groups))
    slot_count = groups * capacity
    grad_scale = 1.0 / math.sqrt(group_rows * dp)
    bf16 = jnp.bfloat16

    swap = [(0, 1), (1, 0)]

    blocked = (chips, CORES, tok_rows, features)
    token_blocks = tokens.reshape(blocked)
    cotangent_blocks = cotangent.reshape(blocked)
    place = core.reshape(1).astype(jnp.int32)
    given, kept, here = swap_operands(
        place, token_blocks, cotangent_blocks, down_proj, up_proj
    )
    got, there = (lax.ppermute(array, "c", swap) for array in (given, here))
    parts = chip_latents(kept, got, here, there)
    latents = lax.psum_scatter(parts, "z", scatter_dimension=0, tiled=True)

    packed = packed_weights(expert_in, expert_out, dp)
    across = lax.axis_size("x")
    neighbours = [packed]
    for step in range(1, across):
        backward = [(i, (i - step) % across) for i in range(across)]
        neighbours.append(lax.ppermute(packed, "x", backward))
    column = lax.axis_index("x").reshape(1).astype(jnp.int32)
    weights = lax.all_gather(arranged(column, neighbours), "y", axis=0, tiled=True)

    to_slot, slot_gate, to_token, gates = slot_tables(routes, gate_weights, groups, capacity)

    def exchange(rows):
        return lax.all_to_all(
            rows.reshape(groups, capacity, rows.shape[1]),
            expert,
            split_axis=0,
            concat_axis=0,
            tiled=True,
        ).reshape(slot_count, rows.shape[1])

    outgoing = dispatched_rows(latents, to_slot, slot_gate)
    result = run_expert(exchange(outgoing), weights)
    returned = exchange(result)
    latents = combined_latents(returned, gates, to_token)
    latents = lax.all_gather(latents, expert, axis=0, tiled=True)
    all_out = latents[:, :latent_width]
    all_grad = latents[:, latent_width:]
    up_part_grad = dot(all_out, cotangent, ROWS)
    down_part_grad = dot(all_grad, tokens, ROWS)
    grads = jnp.concatenate([up_part_grad, down_part_grad], axis=1).astype(bf16)
    grads = grads.reshape(dp, latent_width // dp, 2 * features)
    grads = lax.all_to_all(grads, dp_axes, split_axis=0, concat_axis=0, tiled=True)
    mixed = dot(all_out, up_proj).astype(bf16)
    input_grad = dot(all_grad, down_proj, COLS).astype(bf16)
    summed = shared_sums(grads)
    summed = lax.all_to_all(summed, dp_axes, split_axis=0, concat_axis=0, tiled=True)
    down_grad, up_grad = unpack_grads(summed.reshape(latent_width, 2 * features), grad_scale)
    return mixed, input_grad, down_grad, up_grad


def solution(mesh):
    dp, experts = mesh.devices.shape
    across = math.gcd(dp, ACROSS)
    shape = (dp // across, across, experts // CORES, CORES)
    fine = Mesh(mesh.devices.reshape(shape), ("y", "x", "z", "c"))
    group = ("y", "x")
    expert = ("z", "c")
    in_specs = (
        P(group, expert),
        P(group, expert),
        P(expert, None),
        P(None, expert),
        P(("y", "x", "z", "c"), None),
        P(("y", "x", "z", "c"), None),
        P(expert, group, None),
        P(expert, group, None),
    )
    out_specs = (P(group, expert), P(group, expert), P(expert, None), P(None, expert))
    return jax.shard_map(
        on_device, mesh=fine, in_specs=in_specs, out_specs=out_specs, check_vma=False
    )
```

```python
import functools
import math

import jax
import jax.numpy as jnp
from jax import lax
from jax.experimental import pallas as pl
from jax.experimental.pallas import tpu as pltpu
from jax.sharding import Mesh
from jax.sharding import PartitionSpec as P

TOPK = 4
CORES = 2
CHUNK = 512
ACROSS = 4
SMALL = pltpu.CompilerParams(vmem_limit_bytes=16 * 1024 * 1024)
INNER = (((1,), (0,)), ((), ()))
COLS = (((1,), (1,)), ((), ()))
ROWS = (((0,), (0,)), ((), ()))


def dot(left, right, dims=INNER):
    return lax.dot_general(left, right, dims, preferred_element_type=jnp.float32)


def slot_tables(routes, gate_weights, experts, capacity):
    flat_routes = routes.reshape(-1)
    onehot = (flat_routes[:, None] == jnp.arange(experts, dtype=jnp.int32)[None, :]).astype(
        jnp.int32
    )
    before = jnp.cumsum(onehot, axis=0) - onehot
    position = jnp.sum(before * onehot, axis=1)
    slot = (flat_routes * capacity + position).reshape(routes.shape)
    slot_ids = jnp.arange(experts * capacity, dtype=jnp.int32)
    matches = slot.T[:, None, :] == slot_ids[None, :, None]
    to_slot = jnp.any(matches, axis=0).astype(jnp.bfloat16)
    weighted = jnp.sum(jnp.where(matches, gate_weights.T[:, None, :], 0.0), axis=0)
    slot_gate = jnp.sum(weighted, axis=1, keepdims=True)
    matches = slot[:, :, None] == slot_ids[None, None, :]
    to_token = jnp.any(matches, axis=1).astype(jnp.bfloat16)
    weighted = jnp.sum(jnp.where(matches, gate_weights[:, :, None], 0.0), axis=1)
    gate_high = weighted.astype(jnp.bfloat16)
    gate_low = (weighted - gate_high.astype(jnp.float32)).astype(jnp.bfloat16)
    return to_slot, slot_gate, to_token, jnp.concatenate([gate_high, gate_low], axis=0)


def packed_weights(expert_in, expert_out, dp):
    in_rows, width = expert_in.shape[1:]
    own, latent_width = expert_out.shape[1:]
    hidden = width // 2
    tiles = -(-own // in_rows)
    place = jnp.arange(tiles * dp * in_rows, dtype=jnp.int32)
    tile, device, row = place // (dp * in_rows), place // in_rows % dp, place % in_rows
    unit = tile * in_rows + row
    source = jnp.where(unit < own, device * own + unit, -1)
    pick = (jnp.arange(hidden, dtype=jnp.int32)[:, None] == source[None, :]).astype(jnp.bfloat16)
    both = jnp.concatenate([expert_in[0, :, :hidden], expert_in[0, :, hidden:]], axis=0)
    both = dot(both, pick).astype(jnp.bfloat16)
    rows = jnp.pad(expert_out[0], ((0, tiles * in_rows - own), (0, 0)))
    rows = [rows[t * in_rows : (t + 1) * in_rows] for t in range(tiles)]
    return jnp.concatenate([both[:in_rows], both[in_rows:], *rows], axis=1)


def expert_kernel(rows_ref, gate_ref, up_ref, out_ref, result_ref, sum_out, sum_grad):
    step = pl.program_id(0)
    latent_width = sum_out.shape[1]

    @pl.when(step == 0)
    def _():
        sum_out[...] = jnp.zeros_like(sum_out)
        sum_grad[...] = jnp.zeros_like(sum_grad)

    rows = rows_ref[:, :latent_width]
    gate_part = dot(rows, gate_ref[...])
    up_part = dot(rows, up_ref[...])
    grad_act = dot(rows_ref[:, latent_width:], out_ref[...], COLS)
    sigmoid_gate = jax.nn.sigmoid(gate_part)
    silu = gate_part * sigmoid_gate
    sum_out[...] += dot((silu * up_part).astype(jnp.bfloat16), out_ref[...])
    grad_gate = grad_act * up_part * sigmoid_gate * (1.0 + gate_part * (1.0 - sigmoid_gate))
    sum_grad[...] += dot(grad_gate.astype(jnp.bfloat16), gate_ref[...], COLS)
    sum_grad[...] += dot((grad_act * silu).astype(jnp.bfloat16), up_ref[...], COLS)

    @pl.when(step == pl.num_programs(0) - 1)
    def _():
        result_ref[:, :latent_width] = sum_out[...].astype(jnp.bfloat16)
        result_ref[:, latent_width:] = sum_grad[...].astype(jnp.bfloat16)


def run_expert(rows, weights):
    count, latent_width = rows.shape[0], rows.shape[1] // 2
    padded = weights.shape[1] // 3
    steps = padded // CHUNK
    halves = latent_width // CHUNK
    out_base = 2 * padded // latent_width
    return pl.pallas_call(
        expert_kernel,
        grid=(steps,),
        in_specs=[
            pl.BlockSpec((count, 2 * latent_width), lambda j: (0, 0)),
            pl.BlockSpec((latent_width, CHUNK), lambda j: (0, j)),
            pl.BlockSpec((latent_width, CHUNK), lambda j: (0, steps + j)),
            pl.BlockSpec((CHUNK, latent_width), lambda j: (j % halves, out_base + j // halves)),
        ],
        out_specs=pl.BlockSpec((count, 2 * latent_width), lambda j: (0, 0)),
        out_shape=jax.ShapeDtypeStruct((count, 2 * latent_width), jnp.bfloat16),
        scratch_shapes=[pltpu.VMEM((count, latent_width), jnp.float32)] * 2,
        compiler_params=pltpu.CompilerParams(vmem_limit_bytes=50 * 1024 * 1024),
        cost_estimate=pl.CostEstimate(
            flops=12 * count * latent_width * padded,
            bytes_accessed=2 * (weights.size + 2 * rows.size),
            transcendentals=count * padded,
        ),
    )(rows, weights, weights, weights)


def swap_kernel(
    core_ref, tokens_ref, cotangent_ref, down_ref, up_ref, given_ref, kept_ref, sems
):
    mine = core_ref[0]
    chips, _, _, features = tokens_ref.shape
    latent_width = down_ref.shape[1]
    first, second = pl.ds(0, features), pl.ds(features, features)
    rows = pl.ds(0, chips)
    moves = [
        (tokens_ref.at[:, 1 - mine], given_ref.at[rows, :, first]),
        (cotangent_ref.at[:, 1 - mine], given_ref.at[rows, :, second]),
        (tokens_ref.at[:, mine], kept_ref.at[rows, :, first]),
        (cotangent_ref.at[:, mine], kept_ref.at[rows, :, second]),
    ]
    copies = [pltpu.make_async_copy(*move, sems.at[i]) for i, move in enumerate(moves)]
    for copy in copies:
        copy.start()
    width = 2 * features
    down, up = down_ref[...], up_ref[...].T
    for block in range(latent_width // width):
        here = slice(block * width, (block + 1) * width)
        there = latent_width // width + block
        for result_ref in (given_ref, kept_ref):
            result_ref[chips + block] = down[:, here]
            result_ref[chips + there] = up[:, here]
    for copy in copies:
        copy.wait()


def swap_operands(core, tokens, cotangent, down_proj, up_proj):
    chips, _, tok_rows, features = tokens.shape
    blocks = chips + 2 * (down_proj.shape[1] // (2 * features))
    rows = jax.ShapeDtypeStruct((blocks, tok_rows, 2 * features), jnp.bfloat16)
    return pl.pallas_call(
        swap_kernel,
        in_specs=[pl.BlockSpec(memory_space=pltpu.SMEM)]
        + [pl.BlockSpec(memory_space=pl.ANY)] * 2
        + [pl.BlockSpec(memory_space=pltpu.VMEM)] * 2,
        out_specs=[pl.BlockSpec(memory_space=pltpu.VMEM)] * 2,
        out_shape=[rows, rows],
        scratch_shapes=[pltpu.SemaphoreType.DMA((4,))],
        compiler_params=SMALL,
    )(core, tokens, cotangent, down_proj, up_proj)


def latent_kernel(kept_ref, got_ref, result_ref):
    features = kept_ref.shape[2] // 2
    count, width = result_ref.shape
    latent_width = width // 2
    chips = count // kept_ref.shape[1]
    blocks = latent_width // (2 * features)
    kept = kept_ref[:chips].reshape(count, 2 * features)
    got = got_ref[:chips].reshape(count, 2 * features)
    for half in range(2):
        rows = slice(half * features, (half + 1) * features)
        left = jnp.concatenate([kept[:, rows], got[:, rows]], axis=1)
        for block in range(blocks):
            place = chips + half * blocks + block
            right = jnp.concatenate([kept_ref[place], got_ref[place]], axis=0)
            start = half * latent_width + block * 2 * features
            result_ref[:, start : start + 2 * features] = dot(left, right).astype(jnp.bfloat16)


def chip_latents(kept, got, chips, latent_width):
    count = chips * kept.shape[1]
    return pl.pallas_call(
        latent_kernel,
        out_shape=jax.ShapeDtypeStruct((count, 2 * latent_width), jnp.bfloat16),
        compiler_params=SMALL,
    )(kept, got)


def combine_kernel(returned_ref, gates_ref, spread_ref, result_ref):
    latent_width = returned_ref.shape[1] // 2
    count = spread_ref.shape[0]
    gated = dot(gates_ref[...], returned_ref[:, :latent_width])
    result_ref[:, :latent_width] = (gated[:count] + gated[count:]).astype(jnp.bfloat16)
    result_ref[:, latent_width:] = dot(spread_ref[...], returned_ref[:, latent_width:]).astype(
        jnp.bfloat16
    )


def combined_latents(returned, gates, spread):
    return pl.pallas_call(
        combine_kernel,
        out_shape=jax.ShapeDtypeStruct((spread.shape[0], returned.shape[1]), jnp.bfloat16),
        compiler_params=SMALL,
    )(returned, gates, spread)


def share_kernel(pieces_ref, result_ref):
    summed = jnp.sum(pieces_ref[...].astype(jnp.float32), axis=0).astype(jnp.bfloat16)
    result_ref[...] = jnp.broadcast_to(summed[None], result_ref.shape)


def shared_sums(pieces):
    return pl.pallas_call(
        share_kernel,
        out_shape=jax.ShapeDtypeStruct(pieces.shape, jnp.bfloat16),
        compiler_params=SMALL,
    )(pieces)


def dispatch_kernel(latents_ref, spread_ref, gate_ref, result_ref):
    latent_width = latents_ref.shape[1] // 2
    placed = dot(spread_ref[...], latents_ref[...])
    result_ref[:, :latent_width] = placed[:, :latent_width].astype(jnp.bfloat16)
    result_ref[:, latent_width:] = (placed[:, latent_width:] * gate_ref[...]).astype(jnp.bfloat16)


def dispatched_rows(latents, spread, slot_gate):
    return pl.pallas_call(
        dispatch_kernel,
        out_shape=jax.ShapeDtypeStruct((spread.shape[0], latents.shape[1]), jnp.bfloat16),
        compiler_params=SMALL,
    )(latents, spread, slot_gate)


def arrange_kernel(place_ref, *refs):
    *parts, result_ref = refs
    for step, part in enumerate(parts):
        result_ref[lax.rem(place_ref[0] + step, len(parts))] = part[...]


def arranged(place, parts):
    out = jax.ShapeDtypeStruct((len(parts), *parts[0].shape), parts[0].dtype)
    return pl.pallas_call(
        arrange_kernel,
        in_specs=[pl.BlockSpec(memory_space=pltpu.SMEM)]
        + [pl.BlockSpec(memory_space=pltpu.VMEM)] * len(parts),
        out_shape=out,
        compiler_params=SMALL,
    )(place, *parts).reshape(-1, parts[0].shape[1])


def unpack_kernel(scale, packed_ref, down_ref, up_ref):
    features = up_ref.shape[1]
    up_ref[...] = packed_ref[:, :features].astype(jnp.float32) * scale
    down_ref[...] = packed_ref[:, features:].astype(jnp.float32).T * scale


def unpack_grads(packed, scale):
    latent_width, features = packed.shape[0], packed.shape[1] // 2
    return pl.pallas_call(
        functools.partial(unpack_kernel, scale),
        out_shape=[
            jax.ShapeDtypeStruct((features, latent_width), jnp.float32),
            jax.ShapeDtypeStruct((latent_width, features), jnp.float32),
        ],
        compiler_params=SMALL,
    )(packed)


def on_device(tokens, cotangent, down_proj, up_proj, routes, gate_weights, expert_in, expert_out):
    expert = ("z", "c")
    chips = lax.axis_size("z")
    core = lax.axis_index("c")
    groups = chips * CORES
    dp_axes = ("y", "x")
    dp = lax.axis_size(dp_axes)
    tok_rows = routes.shape[0]
    group_rows = tokens.shape[0]
    features = tokens.shape[1]
    latent_width = down_proj.shape[1]
    capacity = min(tok_rows, tok_rows * TOPK * 5 // (4 * groups))
    slot_count = groups * capacity
    grad_scale = 1.0 / math.sqrt(group_rows * dp)
    bf16 = jnp.bfloat16

    swap = [(0, 1), (1, 0)]

    blocked = (chips, CORES, tok_rows, features)
    token_blocks = tokens.reshape(blocked)
    cotangent_blocks = cotangent.reshape(blocked)
    place = core.reshape(1).astype(jnp.int32)
    given, kept = swap_operands(place, token_blocks, cotangent_blocks, down_proj, up_proj)
    got = lax.ppermute(given, "c", swap)
    parts = chip_latents(kept, got, chips, latent_width)
    latents = lax.psum_scatter(parts, "z", scatter_dimension=0, tiled=True)

    packed = packed_weights(expert_in, expert_out, dp)
    across = lax.axis_size("x")
    neighbours = [packed]
    for step in range(1, across):
        backward = [(i, (i - step) % across) for i in range(across)]
        neighbours.append(lax.ppermute(packed, "x", backward))
    column = lax.axis_index("x").reshape(1).astype(jnp.int32)
    weights = lax.all_gather(arranged(column, neighbours), "y", axis=0, tiled=True)

    to_slot, slot_gate, to_token, gates = lax.optimization_barrier(
        slot_tables(routes, gate_weights, groups, capacity)
    )

    def exchange(rows):
        return lax.all_to_all(
            rows.reshape(groups, capacity, rows.shape[1]),
            expert,
            split_axis=0,
            concat_axis=0,
            tiled=True,
        ).reshape(slot_count, rows.shape[1])

    outgoing = dispatched_rows(latents, to_slot, slot_gate)
    result = run_expert(exchange(outgoing), weights)
    returned = exchange(result)
    latents = combined_latents(returned, gates, to_token)
    latents = lax.all_gather(latents, expert, axis=0, tiled=True)
    all_out = latents[:, :latent_width]
    all_grad = latents[:, latent_width:]
    up_part_grad = dot(all_out, cotangent, ROWS)
    down_part_grad = dot(all_grad, tokens, ROWS)
    grads = jnp.concatenate([up_part_grad, down_part_grad], axis=1).astype(bf16)
    grads = grads.reshape(dp, latent_width // dp, 2 * features)
    grads = lax.all_to_all(grads, dp_axes, split_axis=0, concat_axis=0, tiled=True)
    mixed = dot(all_out, up_proj).astype(bf16)
    input_grad = dot(all_grad, down_proj, COLS).astype(bf16)
    summed = shared_sums(grads)
    summed = lax.all_to_all(summed, dp_axes, split_axis=0, concat_axis=0, tiled=True)
    down_grad, up_grad = unpack_grads(summed.reshape(latent_width, 2 * features), grad_scale)
    return mixed, input_grad, down_grad, up_grad


def solution(mesh):
    dp, experts = mesh.devices.shape
    across = math.gcd(dp, ACROSS)
    shape = (dp // across, across, experts // CORES, CORES)
    fine = Mesh(mesh.devices.reshape(shape), ("y", "x", "z", "c"))
    group = ("y", "x")
    expert = ("z", "c")
    in_specs = (
        P(group, expert),
        P(group, expert),
        P(expert, None),
        P(None, expert),
        P(("y", "x", "z", "c"), None),
        P(("y", "x", "z", "c"), None),
        P(expert, group, None),
        P(expert, group, None),
    )
    out_specs = (P(group, expert), P(group, expert), P(expert, None), P(None, expert))
    return jax.shard_map(
        on_device, mesh=fine, in_specs=in_specs, out_specs=out_specs, check_vma=False
    )
```

```python
import functools
import math

import jax
import jax.numpy as jnp
from jax import lax
from jax.experimental import pallas as pl
from jax.experimental.pallas import tpu as pltpu
from jax.sharding import Mesh
from jax.sharding import PartitionSpec as P

TOPK = 4
CORES = 2
CHUNK = 512
ACROSS = 4
SMALL = pltpu.CompilerParams(vmem_limit_bytes=16 * 1024 * 1024)
LARGE = pltpu.CompilerParams(vmem_limit_bytes=56 * 1024 * 1024)
INNER = (((1,), (0,)), ((), ()))
COLS = (((1,), (1,)), ((), ()))
ROWS = (((0,), (0,)), ((), ()))


def dot(left, right, dims=INNER):
    return lax.dot_general(left, right, dims, preferred_element_type=jnp.float32)


def slot_tables(routes, gate_weights, experts, capacity):
    flat_routes = routes.reshape(-1)
    onehot = (flat_routes[:, None] == jnp.arange(experts, dtype=jnp.int32)[None, :]).astype(
        jnp.int32
    )
    before = jnp.cumsum(onehot, axis=0) - onehot
    position = jnp.sum(before * onehot, axis=1)
    slot = (flat_routes * capacity + position).reshape(routes.shape)
    slot_ids = jnp.arange(experts * capacity, dtype=jnp.int32)
    matches = slot.T[:, None, :] == slot_ids[None, :, None]
    to_slot = jnp.any(matches, axis=0).astype(jnp.bfloat16)
    weighted = jnp.sum(jnp.where(matches, gate_weights.T[:, None, :], 0.0), axis=0)
    slot_gate = jnp.sum(weighted, axis=1, keepdims=True)
    matches = slot[:, :, None] == slot_ids[None, None, :]
    to_token = jnp.any(matches, axis=1).astype(jnp.bfloat16)
    weighted = jnp.sum(jnp.where(matches, gate_weights[:, :, None], 0.0), axis=1)
    gate_high = weighted.astype(jnp.bfloat16)
    gate_low = (weighted - gate_high.astype(jnp.float32)).astype(jnp.bfloat16)
    return to_slot, slot_gate, to_token, jnp.concatenate([gate_high, gate_low], axis=0)


def packed_weights(expert_in, expert_out, dp):
    in_rows, width = expert_in.shape[1:]
    own, latent_width = expert_out.shape[1:]
    hidden = width // 2
    tiles = -(-own // in_rows)
    place = jnp.arange(tiles * dp * in_rows, dtype=jnp.int32)
    tile, device, row = place // (dp * in_rows), place // in_rows % dp, place % in_rows
    unit = tile * in_rows + row
    source = jnp.where(unit < own, device * own + unit, -1)
    pick = (jnp.arange(hidden, dtype=jnp.int32)[:, None] == source[None, :]).astype(jnp.bfloat16)
    both = jnp.concatenate([expert_in[0, :, :hidden], expert_in[0, :, hidden:]], axis=0)
    both = dot(both, pick).astype(jnp.bfloat16)
    rows = jnp.pad(expert_out[0], ((0, tiles * in_rows - own), (0, 0)))
    rows = [rows[t * in_rows : (t + 1) * in_rows] for t in range(tiles)]
    return jnp.concatenate([both[:in_rows], both[in_rows:], *rows], axis=1)


def expert_kernel(rows_ref, gate_ref, up_ref, out_ref, result_ref, sum_out, sum_grad):
    step = pl.program_id(0)
    latent_width = sum_out.shape[1]

    @pl.when(step == 0)
    def _():
        sum_out[...] = jnp.zeros_like(sum_out)
        sum_grad[...] = jnp.zeros_like(sum_grad)

    rows = rows_ref[:, :latent_width]
    gate_part = dot(rows, gate_ref[...])
    up_part = dot(rows, up_ref[...])
    grad_act = dot(rows_ref[:, latent_width:], out_ref[...], COLS)
    sigmoid_gate = jax.nn.sigmoid(gate_part)
    silu = gate_part * sigmoid_gate
    sum_out[...] += dot((silu * up_part).astype(jnp.bfloat16), out_ref[...])
    grad_gate = grad_act * up_part * sigmoid_gate * (1.0 + gate_part * (1.0 - sigmoid_gate))
    sum_grad[...] += dot(grad_gate.astype(jnp.bfloat16), gate_ref[...], COLS)
    sum_grad[...] += dot((grad_act * silu).astype(jnp.bfloat16), up_ref[...], COLS)

    @pl.when(step == pl.num_programs(0) - 1)
    def _():
        result_ref[:, :latent_width] = sum_out[...].astype(jnp.bfloat16)
        result_ref[:, latent_width:] = sum_grad[...].astype(jnp.bfloat16)


def run_expert(rows, weights):
    count, latent_width = rows.shape[0], rows.shape[1] // 2
    padded = weights.shape[1] // 3
    steps = padded // CHUNK
    halves = latent_width // CHUNK
    out_base = 2 * padded // latent_width
    return pl.pallas_call(
        expert_kernel,
        grid=(steps,),
        in_specs=[
            pl.BlockSpec((count, 2 * latent_width), lambda j: (0, 0)),
            pl.BlockSpec((latent_width, CHUNK), lambda j: (0, j)),
            pl.BlockSpec((latent_width, CHUNK), lambda j: (0, steps + j)),
            pl.BlockSpec((CHUNK, latent_width), lambda j: (j % halves, out_base + j // halves)),
        ],
        out_specs=pl.BlockSpec((count, 2 * latent_width), lambda j: (0, 0)),
        out_shape=jax.ShapeDtypeStruct((count, 2 * latent_width), jnp.bfloat16),
        scratch_shapes=[pltpu.VMEM((count, latent_width), jnp.float32)] * 2,
        compiler_params=pltpu.CompilerParams(vmem_limit_bytes=50 * 1024 * 1024),
        cost_estimate=pl.CostEstimate(
            flops=12 * count * latent_width * padded,
            bytes_accessed=2 * (weights.size + 2 * rows.size),
            transcendentals=count * padded,
        ),
    )(rows, weights, weights, weights)


def swap_kernel(
    core_ref, tokens_ref, cotangent_ref, down_ref, up_ref, given_ref, kept_ref, sems
):
    mine = core_ref[0]
    chips, _, _, features = tokens_ref.shape
    latent_width = down_ref.shape[1]
    first, second = pl.ds(0, features), pl.ds(features, features)
    rows = pl.ds(0, chips)
    moves = [
        (tokens_ref.at[:, 1 - mine], given_ref.at[rows, :, first]),
        (cotangent_ref.at[:, 1 - mine], given_ref.at[rows, :, second]),
        (tokens_ref.at[:, mine], kept_ref.at[rows, :, first]),
        (cotangent_ref.at[:, mine], kept_ref.at[rows, :, second]),
    ]
    copies = [pltpu.make_async_copy(*move, sems.at[i]) for i, move in enumerate(moves)]
    for copy in copies:
        copy.start()
    width = 2 * features
    down, up = down_ref[...], up_ref[...].T
    for block in range(latent_width // width):
        here = slice(block * width, (block + 1) * width)
        there = latent_width // width + block
        for result_ref in (given_ref, kept_ref):
            result_ref[chips + block] = down[:, here]
            result_ref[chips + there] = up[:, here]
    for copy in copies:
        copy.wait()


def swap_operands(core, tokens, cotangent, down_proj, up_proj):
    chips, _, tok_rows, features = tokens.shape
    blocks = chips + 2 * (down_proj.shape[1] // (2 * features))
    rows = jax.ShapeDtypeStruct((blocks, tok_rows, 2 * features), jnp.bfloat16)
    return pl.pallas_call(
        swap_kernel,
        in_specs=[pl.BlockSpec(memory_space=pltpu.SMEM)]
        + [pl.BlockSpec(memory_space=pl.ANY)] * 2
        + [pl.BlockSpec(memory_space=pltpu.VMEM)] * 2,
        out_specs=[pl.BlockSpec(memory_space=pltpu.VMEM)] * 2,
        out_shape=[rows, rows],
        scratch_shapes=[pltpu.SemaphoreType.DMA((4,))],
        compiler_params=SMALL,
    )(core, tokens, cotangent, down_proj, up_proj)


def latent_kernel(kept_ref, got_ref, result_ref):
    features = kept_ref.shape[2] // 2
    count, width = result_ref.shape
    latent_width = width // 2
    chips = count // kept_ref.shape[1]
    blocks = latent_width // (2 * features)
    kept = kept_ref[:chips].reshape(count, 2 * features)
    got = got_ref[:chips].reshape(count, 2 * features)
    for half in range(2):
        rows = slice(half * features, (half + 1) * features)
        left = jnp.concatenate([kept[:, rows], got[:, rows]], axis=1)
        for block in range(blocks):
            place = chips + half * blocks + block
            right = jnp.concatenate([kept_ref[place], got_ref[place]], axis=0)
            start = half * latent_width + block * 2 * features
            result_ref[:, start : start + 2 * features] = dot(left, right).astype(jnp.bfloat16)


def chip_latents(kept, got, chips, latent_width):
    count = chips * kept.shape[1]
    return pl.pallas_call(
        latent_kernel,
        out_shape=jax.ShapeDtypeStruct((count, 2 * latent_width), jnp.bfloat16),
        compiler_params=SMALL,
    )(kept, got)


def combine_kernel(returned_ref, gates_ref, spread_ref, result_ref):
    latent_width = returned_ref.shape[1] // 2
    count = spread_ref.shape[0]
    gated = dot(gates_ref[...], returned_ref[:, :latent_width])
    result_ref[:, :latent_width] = (gated[:count] + gated[count:]).astype(jnp.bfloat16)
    result_ref[:, latent_width:] = dot(spread_ref[...], returned_ref[:, latent_width:]).astype(
        jnp.bfloat16
    )


def combined_latents(returned, gates, spread):
    return pl.pallas_call(
        combine_kernel,
        out_shape=jax.ShapeDtypeStruct((spread.shape[0], returned.shape[1]), jnp.bfloat16),
        compiler_params=SMALL,
    )(returned, gates, spread)


def share_kernel(pieces_ref, result_ref):
    summed = jnp.sum(pieces_ref[...].astype(jnp.float32), axis=0).astype(jnp.bfloat16)
    result_ref[...] = jnp.broadcast_to(summed[None], result_ref.shape)


def shared_sums(pieces):
    return pl.pallas_call(
        share_kernel,
        out_shape=jax.ShapeDtypeStruct(pieces.shape, jnp.bfloat16),
        compiler_params=SMALL,
    )(pieces)


def dispatch_kernel(latents_ref, spread_ref, gate_ref, result_ref):
    latent_width = latents_ref.shape[1] // 2
    placed = dot(spread_ref[...], latents_ref[...])
    result_ref[:, :latent_width] = placed[:, :latent_width].astype(jnp.bfloat16)
    result_ref[:, latent_width:] = (placed[:, latent_width:] * gate_ref[...]).astype(jnp.bfloat16)


def dispatched_rows(latents, spread, slot_gate):
    return pl.pallas_call(
        dispatch_kernel,
        out_shape=jax.ShapeDtypeStruct((spread.shape[0], latents.shape[1]), jnp.bfloat16),
        compiler_params=SMALL,
    )(latents, spread, slot_gate)


def arrange_kernel(place_ref, *refs):
    *parts, result_ref = refs
    for step, part in enumerate(parts):
        result_ref[lax.rem(place_ref[0] + step, len(parts))] = part[...]


def arranged(place, parts):
    out = jax.ShapeDtypeStruct((len(parts), *parts[0].shape), parts[0].dtype)
    return pl.pallas_call(
        arrange_kernel,
        in_specs=[pl.BlockSpec(memory_space=pltpu.SMEM)]
        + [pl.BlockSpec(memory_space=pltpu.VMEM)] * len(parts),
        out_shape=out,
        compiler_params=SMALL,
    )(place, *parts).reshape(-1, parts[0].shape[1])


def grads_kernel(latents_ref, kept_ref, got_ref, mine_ref, other_ref):
    count, width = latents_ref.shape
    latent_width = width // 2
    features = kept_ref.shape[2] // 2
    chips = count // kept_ref.shape[1]
    kept = kept_ref[:chips].reshape(count, 2 * features)
    got = got_ref[:chips].reshape(count, 2 * features)
    for half in range(2):
        rows = slice((1 - half) * features, (2 - half) * features)
        here = slice(half * features, (half + 1) * features)
        latents = latents_ref[:, half * latent_width : (half + 1) * latent_width]
        left = jnp.concatenate([kept[:, rows], got[:, rows]], axis=1)
        grad = dot(left, latents, ROWS).astype(jnp.bfloat16)
        mine_ref[here] = grad[:features]
        other_ref[here] = grad[features:]


def projection_grads(latents, kept, got):
    out = jax.ShapeDtypeStruct((kept.shape[2], latents.shape[1] // 2), jnp.bfloat16)
    return pl.pallas_call(
        grads_kernel,
        out_shape=[out] * 2,
        compiler_params=LARGE,
        cost_estimate=pl.CostEstimate(
            flops=2 * latents.size * kept.shape[2],
            bytes_accessed=2 * latents.size,
            transcendentals=0,
        ),
    )(latents, kept, got)


def outputs_kernel(latents_ref, kept_ref, got_ref, mine_ref, other_ref):
    count, width = latents_ref.shape
    latent_width = width // 2
    features = kept_ref.shape[2] // 2
    chips = count // kept_ref.shape[1]
    blocks = latent_width // (2 * features)
    for half in range(2):
        here = slice(half * features, (half + 1) * features)
        latents = latents_ref[:, half * latent_width : (half + 1) * latent_width]
        first = chips + (1 - half) * blocks
        right = [
            jnp.concatenate([ref[first + block] for block in range(blocks)], axis=1)
            for ref in (kept_ref, got_ref)
        ]
        product = dot(latents, jnp.concatenate(right, axis=0), COLS).astype(jnp.bfloat16)
        mine_ref[:, here] = product[:, :features]
        other_ref[:, here] = product[:, features:]


def output_rows(latents, kept, got):
    out = jax.ShapeDtypeStruct((latents.shape[0], kept.shape[2]), jnp.bfloat16)
    return pl.pallas_call(
        outputs_kernel,
        out_shape=[out] * 2,
        compiler_params=SMALL,
        cost_estimate=pl.CostEstimate(
            flops=2 * latents.size * kept.shape[2],
            bytes_accessed=4 * latents.size,
            transcendentals=0,
        ),
    )(latents, kept, got)


def join_kernel(core_ref, mine_ref, got_ref, mixed_ref, input_ref):
    chips, _, tok_rows, features = mixed_ref.shape
    for ref, place in ((mine_ref, core_ref[0]), (got_ref, 1 - core_ref[0])):
        rows = ref[...].reshape(chips, 1, tok_rows, 2 * features)
        mixed_ref[:, pl.ds(place, 1)] = rows[..., :features]
        input_ref[:, pl.ds(place, 1)] = rows[..., features:]


def joined_rows(core, mine, got, blocked):
    out = jax.ShapeDtypeStruct(blocked, jnp.bfloat16)
    return pl.pallas_call(
        join_kernel,
        in_specs=[pl.BlockSpec(memory_space=pltpu.SMEM)]
        + [pl.BlockSpec(memory_space=pltpu.VMEM)] * 2,
        out_shape=[out] * 2,
        compiler_params=SMALL,
        cost_estimate=pl.CostEstimate(
            flops=0, bytes_accessed=8 * mine.size, transcendentals=0
        ),
    )(core, mine, got)


def unpack_kernel(scale, packed_ref, down_ref, up_ref):
    features = up_ref.shape[1]
    up_ref[...] = packed_ref[:features].astype(jnp.float32).T * scale
    down_ref[...] = packed_ref[features:].astype(jnp.float32) * scale


def unpack_grads(packed, scale):
    latent_width, features = packed.shape[1], packed.shape[0] // 2
    return pl.pallas_call(
        functools.partial(unpack_kernel, scale),
        out_shape=[
            jax.ShapeDtypeStruct((features, latent_width), jnp.float32),
            jax.ShapeDtypeStruct((latent_width, features), jnp.float32),
        ],
        compiler_params=SMALL,
    )(packed)


def on_device(tokens, cotangent, down_proj, up_proj, routes, gate_weights, expert_in, expert_out):
    expert = ("z", "c")
    chips = lax.axis_size("z")
    core = lax.axis_index("c")
    groups = chips * CORES
    dp_axes = ("y", "x")
    dp = lax.axis_size(dp_axes)
    tok_rows = routes.shape[0]
    group_rows = tokens.shape[0]
    features = tokens.shape[1]
    latent_width = down_proj.shape[1]
    capacity = min(tok_rows, tok_rows * TOPK * 5 // (4 * groups))
    slot_count = groups * capacity
    grad_scale = 1.0 / math.sqrt(group_rows * dp)

    swap = [(0, 1), (1, 0)]

    blocked = (chips, CORES, tok_rows, features)
    token_blocks = tokens.reshape(blocked)
    cotangent_blocks = cotangent.reshape(blocked)
    place = core.reshape(1).astype(jnp.int32)
    given, kept = swap_operands(place, token_blocks, cotangent_blocks, down_proj, up_proj)
    got = lax.ppermute(given, "c", swap)
    parts = chip_latents(kept, got, chips, latent_width)
    latents = lax.psum_scatter(parts, "z", scatter_dimension=0, tiled=True)

    packed = packed_weights(expert_in, expert_out, dp)
    across = lax.axis_size("x")
    neighbours = [packed]
    for step in range(1, across):
        backward = [(i, (i - step) % across) for i in range(across)]
        neighbours.append(lax.ppermute(packed, "x", backward))
    column = lax.axis_index("x").reshape(1).astype(jnp.int32)
    weights = lax.all_gather(arranged(column, neighbours), "y", axis=0, tiled=True)

    to_slot, slot_gate, to_token, gates = lax.optimization_barrier(
        slot_tables(routes, gate_weights, groups, capacity)
    )

    def exchange(rows):
        return lax.all_to_all(
            rows.reshape(groups, capacity, rows.shape[1]),
            expert,
            split_axis=0,
            concat_axis=0,
            tiled=True,
        ).reshape(slot_count, rows.shape[1])

    outgoing = dispatched_rows(latents, to_slot, slot_gate)
    result = run_expert(exchange(outgoing), weights)
    returned = exchange(result)
    latents = combined_latents(returned, gates, to_token)
    latents = lax.all_gather(latents, "z", axis=0, tiled=True)
    grads, given_grads = projection_grads(latents, kept, got)
    got_grads = lax.ppermute(given_grads, "c", swap)
    outputs, given_outputs = output_rows(latents, kept, got)
    grads = (grads.astype(jnp.float32) + got_grads.astype(jnp.float32)).astype(jnp.bfloat16)
    grads = grads.reshape(dp, 2 * features // dp, latent_width)
    grads = lax.all_to_all(grads, dp_axes, split_axis=0, concat_axis=0, tiled=True)
    got_outputs = lax.ppermute(given_outputs, "c", swap)
    mixed, input_grad = joined_rows(place, outputs, got_outputs, blocked)
    summed = shared_sums(grads)
    summed = lax.all_to_all(summed, dp_axes, split_axis=0, concat_axis=0, tiled=True)
    down_grad, up_grad = unpack_grads(summed.reshape(2 * features, latent_width), grad_scale)
    mixed, input_grad = (rows.reshape(group_rows, features) for rows in (mixed, input_grad))
    return mixed, input_grad, down_grad, up_grad


def solution(mesh):
    dp, experts = mesh.devices.shape
    across = math.gcd(dp, ACROSS)
    shape = (dp // across, across, experts // CORES, CORES)
    fine = Mesh(mesh.devices.reshape(shape), ("y", "x", "z", "c"))
    group = ("y", "x")
    expert = ("z", "c")
    in_specs = (
        P(group, expert),
        P(group, expert),
        P(expert, None),
        P(None, expert),
        P(("y", "x", "z", "c"), None),
        P(("y", "x", "z", "c"), None),
        P(expert, group, None),
        P(expert, group, None),
    )
    out_specs = (P(group, expert), P(group, expert), P(expert, None), P(None, expert))
    return jax.shard_map(
        on_device, mesh=fine, in_specs=in_specs, out_specs=out_specs, check_vma=False
    )
```

```python
import functools
import math

import jax
import jax.numpy as jnp
from jax import lax
from jax.experimental import pallas as pl
from jax.experimental.pallas import tpu as pltpu
from jax.sharding import Mesh
from jax.sharding import PartitionSpec as P

TOPK = 4
CORES = 2
CHUNK = 512
PART = 256
ACROSS = 4
SMALL = pltpu.CompilerParams(vmem_limit_bytes=16 * 1024 * 1024)
INNER = (((1,), (0,)), ((), ()))
COLS = (((1,), (1,)), ((), ()))
ROWS = (((0,), (0,)), ((), ()))


def dot(left, right, dims=INNER):
    return lax.dot_general(left, right, dims, preferred_element_type=jnp.float32)


def slot_tables(routes, gate_weights, experts, capacity):
    flat_routes = routes.reshape(-1)
    onehot = (flat_routes[:, None] == jnp.arange(experts, dtype=jnp.int32)[None, :]).astype(
        jnp.int32
    )
    before = jnp.cumsum(onehot, axis=0) - onehot
    position = jnp.sum(before * onehot, axis=1)
    slot = (flat_routes * capacity + position).reshape(routes.shape)
    slot_ids = jnp.arange(experts * capacity, dtype=jnp.int32)
    matches = slot.T[:, None, :] == slot_ids[None, :, None]
    to_slot = jnp.any(matches, axis=0).astype(jnp.bfloat16)
    weighted = jnp.sum(jnp.where(matches, gate_weights.T[:, None, :], 0.0), axis=0)
    slot_gate = jnp.sum(weighted, axis=1, keepdims=True)
    matches = slot[:, :, None] == slot_ids[None, None, :]
    to_token = jnp.any(matches, axis=1).astype(jnp.bfloat16)
    weighted = jnp.sum(jnp.where(matches, gate_weights[:, :, None], 0.0), axis=1)
    gate_high = weighted.astype(jnp.bfloat16)
    gate_low = (weighted - gate_high.astype(jnp.float32)).astype(jnp.bfloat16)
    return to_slot, slot_gate, to_token, jnp.concatenate([gate_high, gate_low], axis=0)


def packed_weights(expert_in, expert_out, dp):
    in_rows, width = expert_in.shape[1:]
    own, latent_width = expert_out.shape[1:]
    hidden = width // 2
    tiles = -(-own // in_rows)
    place = jnp.arange(tiles * dp * in_rows, dtype=jnp.int32)
    tile, device, row = place // (dp * in_rows), place // in_rows % dp, place % in_rows
    unit = tile * in_rows + row
    source = jnp.where(unit < own, device * own + unit, -1)
    pick = (jnp.arange(hidden, dtype=jnp.int32)[:, None] == source[None, :]).astype(jnp.bfloat16)
    both = jnp.concatenate([expert_in[0, :, :hidden], expert_in[0, :, hidden:]], axis=0)
    both = dot(both, pick).astype(jnp.bfloat16)
    rows = jnp.pad(expert_out[0], ((0, tiles * in_rows - own), (0, 0)))
    rows = [rows[t * in_rows : (t + 1) * in_rows] for t in range(tiles)]
    return jnp.concatenate([both[:in_rows], both[in_rows:], *rows], axis=1)


def expert_kernel(rows_ref, gate_ref, up_ref, out_ref, result_ref, sum_out, sum_grad):
    step = pl.program_id(0)
    latent_width = sum_out.shape[1]

    @pl.when(step == 0)
    def _():
        sum_out[...] = jnp.zeros_like(sum_out)
        sum_grad[...] = jnp.zeros_like(sum_grad)

    rows, grads = rows_ref[:, :latent_width], rows_ref[:, latent_width:]
    products = []
    for part in range(gate_ref.shape[1] // PART):
        here = slice(part * PART, (part + 1) * PART)
        products.append(
            (
                dot(rows, gate_ref[:, here]),
                dot(rows, up_ref[:, here]),
                dot(grads, out_ref[here], COLS),
            )
        )
    results = []
    for gate_part, up_part, grad_act in products:
        sigmoid_gate = jax.nn.sigmoid(gate_part)
        silu = gate_part * sigmoid_gate
        grad_gate = grad_act * up_part * sigmoid_gate * (1.0 + gate_part * (1.0 - sigmoid_gate))
        values = (silu * up_part, grad_gate, grad_act * silu)
        results.append([value.astype(jnp.bfloat16) for value in values])
    activation, grad_gate, grad_upper = (jnp.concatenate(part, axis=1) for part in zip(*results))
    sum_out[...] += dot(activation, out_ref[...])
    sum_grad[...] += dot(grad_gate, gate_ref[...], COLS) + dot(grad_upper, up_ref[...], COLS)

    @pl.when(step == pl.num_programs(0) - 1)
    def _():
        result_ref[:, :latent_width] = sum_out[...].astype(jnp.bfloat16)
        result_ref[:, latent_width:] = sum_grad[...].astype(jnp.bfloat16)


def run_expert(rows, weights):
    count, latent_width = rows.shape[0], rows.shape[1] // 2
    padded = weights.shape[1] // 3
    steps = padded // CHUNK
    halves = latent_width // CHUNK
    out_base = 2 * padded // latent_width
    return pl.pallas_call(
        expert_kernel,
        grid=(steps,),
        in_specs=[
            pl.BlockSpec((count, 2 * latent_width), lambda j: (0, 0)),
            pl.BlockSpec((latent_width, CHUNK), lambda j: (0, j)),
            pl.BlockSpec((latent_width, CHUNK), lambda j: (0, steps + j)),
            pl.BlockSpec((CHUNK, latent_width), lambda j: (j % halves, out_base + j // halves)),
        ],
        out_specs=pl.BlockSpec((count, 2 * latent_width), lambda j: (0, 0)),
        out_shape=jax.ShapeDtypeStruct((count, 2 * latent_width), jnp.bfloat16),
        scratch_shapes=[pltpu.VMEM((count, latent_width), jnp.float32)] * 2,
        compiler_params=pltpu.CompilerParams(vmem_limit_bytes=50 * 1024 * 1024),
        cost_estimate=pl.CostEstimate(
            flops=12 * count * latent_width * padded,
            bytes_accessed=2 * (weights.size + 2 * rows.size),
            transcendentals=count * padded,
        ),
    )(rows, weights, weights, weights)


def swap_kernel(
    core_ref, tokens_ref, cotangent_ref, down_ref, up_ref, given_ref, kept_ref, sems
):
    mine = core_ref[0]
    chips, _, _, features = tokens_ref.shape
    latent_width = down_ref.shape[1]
    first, second = pl.ds(0, features), pl.ds(features, features)
    rows = pl.ds(0, chips)
    moves = [
        (tokens_ref.at[:, 1 - mine], given_ref.at[rows, :, first]),
        (cotangent_ref.at[:, 1 - mine], given_ref.at[rows, :, second]),
        (tokens_ref.at[:, mine], kept_ref.at[rows, :, first]),
        (cotangent_ref.at[:, mine], kept_ref.at[rows, :, second]),
    ]
    copies = [pltpu.make_async_copy(*move, sems.at[i]) for i, move in enumerate(moves)]
    for copy in copies:
        copy.start()
    width = 2 * features
    down, up = down_ref[...], up_ref[...].T
    for block in range(latent_width // width):
        here = slice(block * width, (block + 1) * width)
        there = latent_width // width + block
        for result_ref in (given_ref, kept_ref):
            result_ref[chips + block] = down[:, here]
            result_ref[chips + there] = up[:, here]
    for copy in copies:
        copy.wait()


def swap_operands(core, tokens, cotangent, down_proj, up_proj):
    chips, _, tok_rows, features = tokens.shape
    blocks = chips + 2 * (down_proj.shape[1] // (2 * features))
    rows = jax.ShapeDtypeStruct((blocks, tok_rows, 2 * features), jnp.bfloat16)
    return pl.pallas_call(
        swap_kernel,
        in_specs=[pl.BlockSpec(memory_space=pltpu.SMEM)]
        + [pl.BlockSpec(memory_space=pl.ANY)] * 2
        + [pl.BlockSpec(memory_space=pltpu.VMEM)] * 2,
        out_specs=[pl.BlockSpec(memory_space=pltpu.VMEM)] * 2,
        out_shape=[rows, rows],
        scratch_shapes=[pltpu.SemaphoreType.DMA((4,))],
        compiler_params=SMALL,
    )(core, tokens, cotangent, down_proj, up_proj)


def latent_kernel(kept_ref, got_ref, here_ref, there_ref, result_ref):
    features = kept_ref.shape[2] // 2
    count, width = result_ref.shape
    blocks = here_ref.shape[0] // 2
    kept = kept_ref[...].reshape(count, 2 * features)
    got = got_ref[...].reshape(count, 2 * features)
    for half in range(2):
        rows = slice(half * features, (half + 1) * features)
        left = jnp.concatenate([kept[:, rows], got[:, rows]], axis=1)
        for block in range(blocks):
            place = half * blocks + block
            right = jnp.concatenate([here_ref[place], there_ref[place]], axis=0)
            start = half * (width // 2) + block * 2 * features
            result_ref[:, start : start + 2 * features] = dot(left, right).astype(jnp.bfloat16)


def chip_latents(kept, got, chips, latent_width):
    blocks, tok_rows, width = kept.shape
    last = blocks - chips
    rows = pl.BlockSpec((chips // 2, tok_rows, width), lambda i: (i, 0, 0))
    projections = pl.BlockSpec((last, tok_rows, width), lambda i: (chips // last, 0, 0))
    return pl.pallas_call(
        latent_kernel,
        grid=(2,),
        in_specs=[rows, rows, projections, projections],
        out_specs=pl.BlockSpec((chips // 2 * tok_rows, 2 * latent_width), lambda i: (i, 0)),
        out_shape=jax.ShapeDtypeStruct((chips * tok_rows, 2 * latent_width), jnp.bfloat16),
        compiler_params=SMALL,
    )(kept, got, kept, got)


def combine_kernel(returned_ref, gates_ref, spread_ref, result_ref):
    latent_width = returned_ref.shape[1] // 2
    count = spread_ref.shape[0]
    gated = dot(gates_ref[...], returned_ref[:, :latent_width])
    result_ref[:, :latent_width] = (gated[:count] + gated[count:]).astype(jnp.bfloat16)
    result_ref[:, latent_width:] = dot(spread_ref[...], returned_ref[:, latent_width:]).astype(
        jnp.bfloat16
    )


def combined_latents(returned, gates, spread):
    return pl.pallas_call(
        combine_kernel,
        out_shape=jax.ShapeDtypeStruct((spread.shape[0], returned.shape[1]), jnp.bfloat16),
        compiler_params=SMALL,
    )(returned, gates, spread)


def share_kernel(pieces_ref, result_ref):
    summed = jnp.sum(pieces_ref[...].astype(jnp.float32), axis=0).astype(jnp.bfloat16)
    result_ref[...] = jnp.broadcast_to(summed[None], result_ref.shape)


def shared_sums(pieces):
    return pl.pallas_call(
        share_kernel,
        out_shape=jax.ShapeDtypeStruct(pieces.shape, jnp.bfloat16),
        compiler_params=SMALL,
    )(pieces)


def dispatch_kernel(latents_ref, spread_ref, gate_ref, result_ref):
    latent_width = latents_ref.shape[1] // 2
    placed = dot(spread_ref[...], latents_ref[...])
    result_ref[:, :latent_width] = placed[:, :latent_width].astype(jnp.bfloat16)
    result_ref[:, latent_width:] = (placed[:, latent_width:] * gate_ref[...]).astype(jnp.bfloat16)


def dispatched_rows(latents, spread, slot_gate):
    return pl.pallas_call(
        dispatch_kernel,
        out_shape=jax.ShapeDtypeStruct((spread.shape[0], latents.shape[1]), jnp.bfloat16),
        compiler_params=SMALL,
    )(latents, spread, slot_gate)


def arrange_kernel(place_ref, *refs):
    *parts, result_ref = refs
    for step, part in enumerate(parts):
        result_ref[lax.rem(place_ref[0] + step, len(parts))] = part[...]


def arranged(place, parts):
    out = jax.ShapeDtypeStruct((len(parts), *parts[0].shape), parts[0].dtype)
    return pl.pallas_call(
        arrange_kernel,
        in_specs=[pl.BlockSpec(memory_space=pltpu.SMEM)]
        + [pl.BlockSpec(memory_space=pltpu.VMEM)] * len(parts),
        out_shape=out,
        compiler_params=SMALL,
    )(place, *parts).reshape(-1, parts[0].shape[1])


def unpack_kernel(scale, packed_ref, down_ref, up_ref):
    features = up_ref.shape[1]
    up_ref[...] = packed_ref[:features].astype(jnp.float32).T * scale
    down_ref[...] = packed_ref[features:].astype(jnp.float32) * scale


def unpack_grads(packed, scale):
    latent_width, features = packed.shape[1], packed.shape[0] // 2
    return pl.pallas_call(
        functools.partial(unpack_kernel, scale),
        out_shape=[
            jax.ShapeDtypeStruct((features, latent_width), jnp.float32),
            jax.ShapeDtypeStruct((latent_width, features), jnp.float32),
        ],
        compiler_params=SMALL,
    )(packed)


def on_device(tokens, cotangent, down_proj, up_proj, routes, gate_weights, expert_in, expert_out):
    expert = ("z", "c")
    chips = lax.axis_size("z")
    core = lax.axis_index("c")
    groups = chips * CORES
    dp_axes = ("y", "x")
    dp = lax.axis_size(dp_axes)
    tok_rows = routes.shape[0]
    group_rows = tokens.shape[0]
    features = tokens.shape[1]
    latent_width = down_proj.shape[1]
    capacity = min(tok_rows, tok_rows * TOPK * 5 // (4 * groups))
    slot_count = groups * capacity
    grad_scale = 1.0 / math.sqrt(group_rows * dp)
    bf16 = jnp.bfloat16

    swap = [(0, 1), (1, 0)]

    blocked = (chips, CORES, tok_rows, features)
    token_blocks = tokens.reshape(blocked)
    cotangent_blocks = cotangent.reshape(blocked)
    place = core.reshape(1).astype(jnp.int32)
    given, kept = swap_operands(place, token_blocks, cotangent_blocks, down_proj, up_proj)
    got = lax.ppermute(given, "c", swap)
    parts = chip_latents(kept, got, chips, latent_width)
    latents = lax.psum_scatter(parts, "z", scatter_dimension=0, tiled=True)

    packed = packed_weights(expert_in, expert_out, dp)
    across = lax.axis_size("x")
    neighbours = [packed]
    for step in range(1, across):
        backward = [(i, (i - step) % across) for i in range(across)]
        neighbours.append(lax.ppermute(packed, "x", backward))
    column = lax.axis_index("x").reshape(1).astype(jnp.int32)
    weights = lax.all_gather(arranged(column, neighbours), "y", axis=0, tiled=True)

    to_slot, slot_gate, to_token, gates = lax.optimization_barrier(
        slot_tables(routes, gate_weights, groups, capacity)
    )

    def exchange(rows):
        return lax.all_to_all(
            rows.reshape(groups, capacity, rows.shape[1]),
            expert,
            split_axis=0,
            concat_axis=0,
            tiled=True,
        ).reshape(slot_count, rows.shape[1])

    outgoing = dispatched_rows(latents, to_slot, slot_gate)
    result = run_expert(exchange(outgoing), weights)
    returned = exchange(result)
    latents = combined_latents(returned, gates, to_token)
    latents = lax.all_gather(latents, expert, axis=0, tiled=True)
    all_out = latents[:, :latent_width]
    all_grad = latents[:, latent_width:]
    up_part_grad = dot(cotangent, all_out, ROWS)
    down_part_grad = dot(tokens, all_grad, ROWS)
    grads = jnp.concatenate([up_part_grad, down_part_grad], axis=0).astype(bf16)
    grads = grads.reshape(dp, 2 * features // dp, latent_width)
    grads = lax.all_to_all(grads, dp_axes, split_axis=0, concat_axis=0, tiled=True)
    mixed = dot(all_out, up_proj).astype(bf16)
    input_grad = dot(all_grad, down_proj, COLS).astype(bf16)
    summed = shared_sums(grads)
    summed = lax.all_to_all(summed, dp_axes, split_axis=0, concat_axis=0, tiled=True)
    down_grad, up_grad = unpack_grads(summed.reshape(2 * features, latent_width), grad_scale)
    return mixed, input_grad, down_grad, up_grad


def solution(mesh):
    dp, experts = mesh.devices.shape
    across = math.gcd(dp, ACROSS)
    shape = (dp // across, across, experts // CORES, CORES)
    fine = Mesh(mesh.devices.reshape(shape), ("y", "x", "z", "c"))
    group = ("y", "x")
    expert = ("z", "c")
    in_specs = (
        P(group, expert),
        P(group, expert),
        P(expert, None),
        P(None, expert),
        P(("y", "x", "z", "c"), None),
        P(("y", "x", "z", "c"), None),
        P(expert, group, None),
        P(expert, group, None),
    )
    out_specs = (P(group, expert), P(group, expert), P(expert, None), P(None, expert))
    return jax.shard_map(
        on_device, mesh=fine, in_specs=in_specs, out_specs=out_specs, check_vma=False
    )
```

```python
import functools
import math

import jax
import jax.numpy as jnp
from jax import lax
from jax.experimental import pallas as pl
from jax.experimental.pallas import tpu as pltpu
from jax.sharding import Mesh
from jax.sharding import PartitionSpec as P

TOPK = 4
CORES = 2
CHUNK = 512
PART = 256
ACROSS = 4
SMALL = pltpu.CompilerParams(vmem_limit_bytes=16 * 1024 * 1024)
INNER = (((1,), (0,)), ((), ()))
COLS = (((1,), (1,)), ((), ()))
ROWS = (((0,), (0,)), ((), ()))


def dot(left, right, dims=INNER):
    return lax.dot_general(left, right, dims, preferred_element_type=jnp.float32)


def slot_tables(routes, gate_weights, experts, capacity):
    flat_routes = routes.reshape(-1)
    onehot = (flat_routes[:, None] == jnp.arange(experts, dtype=jnp.int32)[None, :]).astype(
        jnp.int32
    )
    before = jnp.cumsum(onehot, axis=0) - onehot
    position = jnp.sum(before * onehot, axis=1)
    slot = (flat_routes * capacity + position).reshape(routes.shape)
    slot_ids = jnp.arange(experts * capacity, dtype=jnp.int32)
    matches = slot.T[:, None, :] == slot_ids[None, :, None]
    to_slot = jnp.any(matches, axis=0).astype(jnp.bfloat16)
    weighted = jnp.sum(jnp.where(matches, gate_weights.T[:, None, :], 0.0), axis=0)
    slot_gate = jnp.sum(weighted, axis=1, keepdims=True)
    matches = slot[:, :, None] == slot_ids[None, None, :]
    to_token = jnp.any(matches, axis=1).astype(jnp.bfloat16)
    weighted = jnp.sum(jnp.where(matches, gate_weights[:, :, None], 0.0), axis=1)
    gate_high = weighted.astype(jnp.bfloat16)
    gate_low = (weighted - gate_high.astype(jnp.float32)).astype(jnp.bfloat16)
    return to_slot, slot_gate, to_token, jnp.concatenate([gate_high, gate_low], axis=0)


def packed_weights(expert_in, expert_out, dp):
    in_rows, width = expert_in.shape[1:]
    own, latent_width = expert_out.shape[1:]
    hidden = width // 2
    tiles = -(-own // in_rows)
    place = jnp.arange(tiles * dp * in_rows, dtype=jnp.int32)
    tile, device, row = place // (dp * in_rows), place // in_rows % dp, place % in_rows
    unit = tile * in_rows + row
    source = jnp.where(unit < own, device * own + unit, -1)
    pick = (jnp.arange(hidden, dtype=jnp.int32)[:, None] == source[None, :]).astype(jnp.bfloat16)
    both = jnp.concatenate([expert_in[0, :, :hidden], expert_in[0, :, hidden:]], axis=0)
    both = dot(both, pick).astype(jnp.bfloat16)
    rows = jnp.pad(expert_out[0], ((0, tiles * in_rows - own), (0, 0)))
    rows = [rows[t * in_rows : (t + 1) * in_rows] for t in range(tiles)]
    return jnp.concatenate([both[:in_rows], both[in_rows:], *rows], axis=1)


def expert_kernel(rows_ref, gate_ref, up_ref, out_ref, result_ref, sum_out, sum_grad):
    step = pl.program_id(0)
    latent_width = sum_out.shape[1]

    @pl.when(step == 0)
    def _():
        sum_out[...] = jnp.zeros_like(sum_out)
        sum_grad[...] = jnp.zeros_like(sum_grad)

    rows, grads = rows_ref[:, :latent_width], rows_ref[:, latent_width:]
    products = []
    for part in range(gate_ref.shape[1] // PART):
        here = slice(part * PART, (part + 1) * PART)
        products.append(
            (
                dot(rows, gate_ref[:, here]),
                dot(rows, up_ref[:, here]),
                dot(grads, out_ref[here], COLS),
            )
        )
    results = []
    for gate_part, up_part, grad_act in products:
        sigmoid_gate = jax.nn.sigmoid(gate_part)
        silu = gate_part * sigmoid_gate
        grad_gate = grad_act * up_part * sigmoid_gate * (1.0 + gate_part * (1.0 - sigmoid_gate))
        values = (silu * up_part, grad_gate, grad_act * silu)
        results.append([value.astype(jnp.bfloat16) for value in values])
    activation, grad_gate, grad_upper = (jnp.concatenate(part, axis=1) for part in zip(*results))
    sum_out[...] += dot(activation, out_ref[...])
    sum_grad[...] += dot(grad_gate, gate_ref[...], COLS) + dot(grad_upper, up_ref[...], COLS)

    @pl.when(step == pl.num_programs(0) - 1)
    def _():
        result_ref[:, :latent_width] = sum_out[...].astype(jnp.bfloat16)
        result_ref[:, latent_width:] = sum_grad[...].astype(jnp.bfloat16)


def run_expert(rows, weights):
    count, latent_width = rows.shape[0], rows.shape[1] // 2
    padded = weights.shape[1] // 3
    steps = padded // CHUNK
    halves = latent_width // CHUNK
    out_base = 2 * padded // latent_width
    return pl.pallas_call(
        expert_kernel,
        grid=(steps,),
        in_specs=[
            pl.BlockSpec((count, 2 * latent_width), lambda j: (0, 0)),
            pl.BlockSpec((latent_width, CHUNK), lambda j: (0, j)),
            pl.BlockSpec((latent_width, CHUNK), lambda j: (0, steps + j)),
            pl.BlockSpec((CHUNK, latent_width), lambda j: (j % halves, out_base + j // halves)),
        ],
        out_specs=pl.BlockSpec((count, 2 * latent_width), lambda j: (0, 0)),
        out_shape=jax.ShapeDtypeStruct((count, 2 * latent_width), jnp.bfloat16),
        scratch_shapes=[pltpu.VMEM((count, latent_width), jnp.float32)] * 2,
        compiler_params=pltpu.CompilerParams(vmem_limit_bytes=50 * 1024 * 1024),
        cost_estimate=pl.CostEstimate(
            flops=12 * count * latent_width * padded,
            bytes_accessed=2 * (weights.size + 2 * rows.size),
            transcendentals=count * padded,
        ),
    )(rows, weights, weights, weights)


def swap_kernel(
    core_ref, tokens_ref, cotangent_ref, down_ref, up_ref, given_ref, kept_ref, sems
):
    mine = core_ref[0]
    chips, _, _, features = tokens_ref.shape
    latent_width = down_ref.shape[1]
    first, second = pl.ds(0, features), pl.ds(features, features)
    rows = pl.ds(0, chips)
    moves = [
        (tokens_ref.at[:, 1 - mine], given_ref.at[rows, :, first]),
        (cotangent_ref.at[:, 1 - mine], given_ref.at[rows, :, second]),
        (tokens_ref.at[:, mine], kept_ref.at[rows, :, first]),
        (cotangent_ref.at[:, mine], kept_ref.at[rows, :, second]),
    ]
    copies = [pltpu.make_async_copy(*move, sems.at[i]) for i, move in enumerate(moves)]
    for copy in copies:
        copy.start()
    width = 2 * features
    down, up = down_ref[...], up_ref[...].T
    for block in range(latent_width // width):
        here = slice(block * width, (block + 1) * width)
        there = latent_width // width + block
        for result_ref in (given_ref, kept_ref):
            result_ref[chips + block] = down[:, here]
            result_ref[chips + there] = up[:, here]
    for copy in copies:
        copy.wait()


def swap_operands(core, tokens, cotangent, down_proj, up_proj):
    chips, _, tok_rows, features = tokens.shape
    blocks = chips + 2 * (down_proj.shape[1] // (2 * features))
    rows = jax.ShapeDtypeStruct((blocks, tok_rows, 2 * features), jnp.bfloat16)
    return pl.pallas_call(
        swap_kernel,
        in_specs=[pl.BlockSpec(memory_space=pltpu.SMEM)]
        + [pl.BlockSpec(memory_space=pl.ANY)] * 2
        + [pl.BlockSpec(memory_space=pltpu.VMEM)] * 2,
        out_specs=[pl.BlockSpec(memory_space=pltpu.VMEM)] * 2,
        out_shape=[rows, rows],
        scratch_shapes=[pltpu.SemaphoreType.DMA((4,))],
        compiler_params=SMALL,
    )(core, tokens, cotangent, down_proj, up_proj)


def latent_kernel(kept_ref, got_ref, here_ref, there_ref, result_ref):
    features = kept_ref.shape[2] // 2
    count, width = result_ref.shape
    blocks = here_ref.shape[0] // 2
    kept = kept_ref[...].reshape(count, 2 * features)
    got = got_ref[...].reshape(count, 2 * features)
    for half in range(2):
        rows = slice(half * features, (half + 1) * features)
        left = jnp.concatenate([kept[:, rows], got[:, rows]], axis=1)
        for block in range(blocks):
            place = half * blocks + block
            right = jnp.concatenate([here_ref[place], there_ref[place]], axis=0)
            start = half * (width // 2) + block * 2 * features
            result_ref[:, start : start + 2 * features] = dot(left, right).astype(jnp.bfloat16)


def chip_latents(kept, got, chips, latent_width):
    blocks, tok_rows, width = kept.shape
    last = blocks - chips
    rows = pl.BlockSpec((chips // 2, tok_rows, width), lambda i: (i, 0, 0))
    projections = pl.BlockSpec((last, tok_rows, width), lambda i: (chips // last, 0, 0))
    return pl.pallas_call(
        latent_kernel,
        grid=(2,),
        in_specs=[rows, rows, projections, projections],
        out_specs=pl.BlockSpec((chips // 2 * tok_rows, 2 * latent_width), lambda i: (i, 0)),
        out_shape=jax.ShapeDtypeStruct((chips * tok_rows, 2 * latent_width), jnp.bfloat16),
        compiler_params=SMALL,
    )(kept, got, kept, got)


def combine_kernel(returned_ref, gates_ref, spread_ref, result_ref):
    latent_width = returned_ref.shape[1] // 2
    count = spread_ref.shape[0]
    gated = dot(gates_ref[...], returned_ref[:, :latent_width])
    result_ref[:, :latent_width] = (gated[:count] + gated[count:]).astype(jnp.bfloat16)
    result_ref[:, latent_width:] = dot(spread_ref[...], returned_ref[:, latent_width:]).astype(
        jnp.bfloat16
    )


def combined_latents(returned, gates, spread):
    return pl.pallas_call(
        combine_kernel,
        out_shape=jax.ShapeDtypeStruct((spread.shape[0], returned.shape[1]), jnp.bfloat16),
        compiler_params=SMALL,
    )(returned, gates, spread)


def share_kernel(pieces_ref, result_ref):
    summed = jnp.sum(pieces_ref[...].astype(jnp.float32), axis=0).astype(jnp.bfloat16)
    result_ref[...] = jnp.broadcast_to(summed[None], result_ref.shape)


def shared_sums(pieces):
    return pl.pallas_call(
        share_kernel,
        out_shape=jax.ShapeDtypeStruct(pieces.shape, jnp.bfloat16),
        compiler_params=SMALL,
    )(pieces)


def dispatch_kernel(latents_ref, spread_ref, gate_ref, result_ref):
    latent_width = latents_ref.shape[1] // 2
    placed = dot(spread_ref[...], latents_ref[...])
    result_ref[:, :latent_width] = placed[:, :latent_width].astype(jnp.bfloat16)
    result_ref[:, latent_width:] = (placed[:, latent_width:] * gate_ref[...]).astype(jnp.bfloat16)


def dispatched_rows(latents, spread, slot_gate):
    return pl.pallas_call(
        dispatch_kernel,
        out_shape=jax.ShapeDtypeStruct((spread.shape[0], latents.shape[1]), jnp.bfloat16),
        compiler_params=SMALL,
    )(latents, spread, slot_gate)


def arrange_kernel(place_ref, *refs):
    *parts, result_ref = refs
    for step, part in enumerate(parts):
        result_ref[lax.rem(place_ref[0] + step, len(parts))] = part[...]


def arranged(place, parts):
    out = jax.ShapeDtypeStruct((len(parts), *parts[0].shape), parts[0].dtype)
    return pl.pallas_call(
        arrange_kernel,
        in_specs=[pl.BlockSpec(memory_space=pltpu.SMEM)]
        + [pl.BlockSpec(memory_space=pltpu.VMEM)] * len(parts),
        out_shape=out,
        compiler_params=SMALL,
    )(place, *parts).reshape(-1, parts[0].shape[1])


def unpack_kernel(scale, packed_ref, down_ref, up_ref):
    features = up_ref.shape[1]
    up_ref[...] = packed_ref[:features].astype(jnp.float32).T * scale
    down_ref[...] = packed_ref[features:].astype(jnp.float32) * scale


def unpack_grads(packed, scale):
    latent_width, features = packed.shape[1], packed.shape[0] // 2
    return pl.pallas_call(
        functools.partial(unpack_kernel, scale),
        out_shape=[
            jax.ShapeDtypeStruct((features, latent_width), jnp.float32),
            jax.ShapeDtypeStruct((latent_width, features), jnp.float32),
        ],
        compiler_params=SMALL,
    )(packed)


def on_device(tokens, cotangent, down_proj, up_proj, routes, gate_weights, expert_in, expert_out):
    expert = ("z", "c")
    chips = lax.axis_size("z")
    core = lax.axis_index("c")
    groups = chips * CORES
    dp_axes = ("y", "x")
    dp = lax.axis_size(dp_axes)
    tok_rows = routes.shape[0]
    group_rows = tokens.shape[0]
    features = tokens.shape[1]
    latent_width = down_proj.shape[1]
    capacity = min(tok_rows, tok_rows * TOPK * 5 // (4 * groups))
    slot_count = groups * capacity
    grad_scale = 1.0 / math.sqrt(group_rows * dp)
    bf16 = jnp.bfloat16

    swap = [(0, 1), (1, 0)]

    blocked = (chips, CORES, tok_rows, features)
    token_blocks = tokens.reshape(blocked)
    cotangent_blocks = cotangent.reshape(blocked)
    place = core.reshape(1).astype(jnp.int32)
    packed, place = lax.optimization_barrier((packed_weights(expert_in, expert_out, dp), place))
    given, kept = swap_operands(place, token_blocks, cotangent_blocks, down_proj, up_proj)
    got = lax.ppermute(given, "c", swap)
    parts = chip_latents(kept, got, chips, latent_width)
    packed, parts = lax.optimization_barrier((packed, parts))
    latents = lax.psum_scatter(parts, "z", scatter_dimension=0, tiled=True)

    across = lax.axis_size("x")
    neighbours = [packed]
    for step in range(1, across):
        backward = [(i, (i - step) % across) for i in range(across)]
        neighbours.append(lax.ppermute(packed, "x", backward))
    column = lax.axis_index("x").reshape(1).astype(jnp.int32)
    weights = lax.all_gather(arranged(column, neighbours), "y", axis=0, tiled=True)

    to_slot, slot_gate, to_token, gates = lax.optimization_barrier(
        slot_tables(routes, gate_weights, groups, capacity)
    )

    def exchange(rows):
        return lax.all_to_all(
            rows.reshape(groups, capacity, rows.shape[1]),
            expert,
            split_axis=0,
            concat_axis=0,
            tiled=True,
        ).reshape(slot_count, rows.shape[1])

    outgoing = dispatched_rows(latents, to_slot, slot_gate)
    result = run_expert(exchange(outgoing), weights)
    returned = exchange(result)
    latents = combined_latents(returned, gates, to_token)
    latents = lax.all_gather(latents, expert, axis=0, tiled=True)
    all_out = latents[:, :latent_width]
    all_grad = latents[:, latent_width:]
    up_part_grad = dot(cotangent, all_out, ROWS)
    down_part_grad = dot(tokens, all_grad, ROWS)
    grads = jnp.concatenate([up_part_grad, down_part_grad], axis=0).astype(bf16)
    grads = grads.reshape(dp, 2 * features // dp, latent_width)
    grads = lax.all_to_all(grads, dp_axes, split_axis=0, concat_axis=0, tiled=True)
    mixed = dot(all_out, up_proj).astype(bf16)
    input_grad = dot(all_grad, down_proj, COLS).astype(bf16)
    summed = shared_sums(grads)
    summed = lax.all_to_all(summed, dp_axes, split_axis=0, concat_axis=0, tiled=True)
    down_grad, up_grad = unpack_grads(summed.reshape(2 * features, latent_width), grad_scale)
    return mixed, input_grad, down_grad, up_grad


def solution(mesh):
    dp, experts = mesh.devices.shape
    across = math.gcd(dp, ACROSS)
    shape = (dp // across, across, experts // CORES, CORES)
    fine = Mesh(mesh.devices.reshape(shape), ("y", "x", "z", "c"))
    group = ("y", "x")
    expert = ("z", "c")
    in_specs = (
        P(group, expert),
        P(group, expert),
        P(expert, None),
        P(None, expert),
        P(("y", "x", "z", "c"), None),
        P(("y", "x", "z", "c"), None),
        P(expert, group, None),
        P(expert, group, None),
    )
    out_specs = (P(group, expert), P(group, expert), P(expert, None), P(None, expert))
    return jax.shard_map(
        on_device, mesh=fine, in_specs=in_specs, out_specs=out_specs, check_vma=False
    )
```

```python
import functools
import math

import jax
import jax.numpy as jnp
from jax import lax
from jax.experimental import pallas as pl
from jax.experimental.pallas import tpu as pltpu
from jax.sharding import Mesh
from jax.sharding import PartitionSpec as P

TOPK = 4
CORES = 2
CHUNK = 512
PART = 256
ACROSS = 4
SMALL = pltpu.CompilerParams(vmem_limit_bytes=16 * 1024 * 1024)
INNER = (((1,), (0,)), ((), ()))
COLS = (((1,), (1,)), ((), ()))
ROWS = (((0,), (0,)), ((), ()))


def dot(left, right, dims=INNER):
    return lax.dot_general(left, right, dims, preferred_element_type=jnp.float32)


def slot_tables(routes, gate_weights, experts, capacity):
    flat_routes = routes.reshape(-1)
    onehot = (flat_routes[:, None] == jnp.arange(experts, dtype=jnp.int32)[None, :]).astype(
        jnp.int32
    )
    before = jnp.cumsum(onehot, axis=0) - onehot
    position = jnp.sum(before * onehot, axis=1)
    slot = (flat_routes * capacity + position).reshape(routes.shape)
    slot_ids = jnp.arange(experts * capacity, dtype=jnp.int32)
    matches = slot.T[:, None, :] == slot_ids[None, :, None]
    to_slot = jnp.any(matches, axis=0).astype(jnp.bfloat16)
    weighted = jnp.sum(jnp.where(matches, gate_weights.T[:, None, :], 0.0), axis=0)
    slot_gate = jnp.sum(weighted, axis=1, keepdims=True)
    matches = slot[:, :, None] == slot_ids[None, None, :]
    to_token = jnp.any(matches, axis=1).astype(jnp.bfloat16)
    weighted = jnp.sum(jnp.where(matches, gate_weights[:, :, None], 0.0), axis=1)
    gate_high = weighted.astype(jnp.bfloat16)
    gate_low = (weighted - gate_high.astype(jnp.float32)).astype(jnp.bfloat16)
    return to_slot, slot_gate, to_token, jnp.concatenate([gate_high, gate_low], axis=0)


def regrouped(expert_in, expert_out, dp):
    in_rows, width = expert_in.shape[1:]
    own, latent_width = expert_out.shape[1:]
    hidden = width // 2
    tiles = -(-own // in_rows)
    place = jnp.arange(tiles * dp * in_rows, dtype=jnp.int32)
    tile, device, row = place // (dp * in_rows), place // in_rows % dp, place % in_rows
    unit = tile * in_rows + row
    source = jnp.where(unit < own, device * own + unit, -1)
    pick = (jnp.arange(hidden, dtype=jnp.int32)[:, None] == source[None, :]).astype(jnp.bfloat16)
    both = jnp.concatenate([expert_in[0, :, :hidden], expert_in[0, :, hidden:]], axis=0)
    both = dot(both, pick).astype(jnp.bfloat16)
    return both


def packed_weights(both, expert_out):
    in_rows = both.shape[0] // 2
    own = expert_out.shape[1]
    tiles = -(-own // in_rows)
    rows = jnp.pad(expert_out[0], ((0, tiles * in_rows - own), (0, 0)))
    rows = [rows[t * in_rows : (t + 1) * in_rows] for t in range(tiles)]
    return jnp.concatenate([both[:in_rows], both[in_rows:], *rows], axis=1)


def expert_kernel(rows_ref, gate_ref, up_ref, out_ref, result_ref, sum_out, sum_grad):
    step = pl.program_id(0)
    latent_width = sum_out.shape[1]

    @pl.when(step == 0)
    def _():
        sum_out[...] = jnp.zeros_like(sum_out)
        sum_grad[...] = jnp.zeros_like(sum_grad)

    rows, grads = rows_ref[:, :latent_width], rows_ref[:, latent_width:]
    products = []
    for part in range(gate_ref.shape[1] // PART):
        here = slice(part * PART, (part + 1) * PART)
        products.append(
            (
                dot(rows, gate_ref[:, here]),
                dot(rows, up_ref[:, here]),
                dot(grads, out_ref[here], COLS),
            )
        )
    results = []
    for gate_part, up_part, grad_act in products:
        sigmoid_gate = jax.nn.sigmoid(gate_part)
        silu = gate_part * sigmoid_gate
        grad_gate = grad_act * up_part * sigmoid_gate * (1.0 + gate_part * (1.0 - sigmoid_gate))
        values = (silu * up_part, grad_gate, grad_act * silu)
        results.append([value.astype(jnp.bfloat16) for value in values])
    activation, grad_gate, grad_upper = (jnp.concatenate(part, axis=1) for part in zip(*results))
    sum_out[...] += dot(activation, out_ref[...])
    sum_grad[...] += dot(grad_gate, gate_ref[...], COLS) + dot(grad_upper, up_ref[...], COLS)

    @pl.when(step == pl.num_programs(0) - 1)
    def _():
        result_ref[:, :latent_width] = sum_out[...].astype(jnp.bfloat16)
        result_ref[:, latent_width:] = sum_grad[...].astype(jnp.bfloat16)


def run_expert(rows, weights):
    count, latent_width = rows.shape[0], rows.shape[1] // 2
    padded = weights.shape[1] // 3
    steps = padded // CHUNK
    halves = latent_width // CHUNK
    out_base = 2 * padded // latent_width
    return pl.pallas_call(
        expert_kernel,
        grid=(steps,),
        in_specs=[
            pl.BlockSpec((count, 2 * latent_width), lambda j: (0, 0)),
            pl.BlockSpec((latent_width, CHUNK), lambda j: (0, j)),
            pl.BlockSpec((latent_width, CHUNK), lambda j: (0, steps + j)),
            pl.BlockSpec((CHUNK, latent_width), lambda j: (j % halves, out_base + j // halves)),
        ],
        out_specs=pl.BlockSpec((count, 2 * latent_width), lambda j: (0, 0)),
        out_shape=jax.ShapeDtypeStruct((count, 2 * latent_width), jnp.bfloat16),
        scratch_shapes=[pltpu.VMEM((count, latent_width), jnp.float32)] * 2,
        compiler_params=pltpu.CompilerParams(vmem_limit_bytes=50 * 1024 * 1024),
        cost_estimate=pl.CostEstimate(
            flops=12 * count * latent_width * padded,
            bytes_accessed=2 * (weights.size + 2 * rows.size),
            transcendentals=count * padded,
        ),
    )(rows, weights, weights, weights)


def swap_kernel(
    core_ref, tokens_ref, cotangent_ref, down_ref, up_ref, given_ref, kept_ref, sems
):
    mine = core_ref[0]
    chips, _, _, features = tokens_ref.shape
    latent_width = down_ref.shape[1]
    first, second = pl.ds(0, features), pl.ds(features, features)
    rows = pl.ds(0, chips)
    moves = [
        (tokens_ref.at[:, 1 - mine], given_ref.at[rows, :, first]),
        (cotangent_ref.at[:, 1 - mine], given_ref.at[rows, :, second]),
        (tokens_ref.at[:, mine], kept_ref.at[rows, :, first]),
        (cotangent_ref.at[:, mine], kept_ref.at[rows, :, second]),
    ]
    copies = [pltpu.make_async_copy(*move, sems.at[i]) for i, move in enumerate(moves)]
    for copy in copies:
        copy.start()
    width = 2 * features
    down, up = down_ref[...], up_ref[...].T
    for block in range(latent_width // width):
        here = slice(block * width, (block + 1) * width)
        there = latent_width // width + block
        for result_ref in (given_ref, kept_ref):
            result_ref[chips + block] = down[:, here]
            result_ref[chips + there] = up[:, here]
    for copy in copies:
        copy.wait()


def swap_operands(core, tokens, cotangent, down_proj, up_proj):
    chips, _, tok_rows, features = tokens.shape
    blocks = chips + 2 * (down_proj.shape[1] // (2 * features))
    rows = jax.ShapeDtypeStruct((blocks, tok_rows, 2 * features), jnp.bfloat16)
    return pl.pallas_call(
        swap_kernel,
        in_specs=[pl.BlockSpec(memory_space=pltpu.SMEM)]
        + [pl.BlockSpec(memory_space=pl.ANY)] * 2
        + [pl.BlockSpec(memory_space=pltpu.VMEM)] * 2,
        out_specs=[pl.BlockSpec(memory_space=pltpu.VMEM)] * 2,
        out_shape=[rows, rows],
        scratch_shapes=[pltpu.SemaphoreType.DMA((4,))],
        compiler_params=SMALL,
    )(core, tokens, cotangent, down_proj, up_proj)


def latent_kernel(kept_ref, got_ref, here_ref, there_ref, result_ref):
    features = kept_ref.shape[2] // 2
    count, width = result_ref.shape
    blocks = here_ref.shape[0] // 2
    kept = kept_ref[...].reshape(count, 2 * features)
    got = got_ref[...].reshape(count, 2 * features)
    for half in range(2):
        rows = slice(half * features, (half + 1) * features)
        left = jnp.concatenate([kept[:, rows], got[:, rows]], axis=1)
        for block in range(blocks):
            place = half * blocks + block
            right = jnp.concatenate([here_ref[place], there_ref[place]], axis=0)
            start = half * (width // 2) + block * 2 * features
            result_ref[:, start : start + 2 * features] = dot(left, right).astype(jnp.bfloat16)


def chip_latents(kept, got, chips, latent_width):
    blocks, tok_rows, width = kept.shape
    last = blocks - chips
    rows = pl.BlockSpec((chips // 2, tok_rows, width), lambda i: (i, 0, 0))
    projections = pl.BlockSpec((last, tok_rows, width), lambda i: (chips // last, 0, 0))
    return pl.pallas_call(
        latent_kernel,
        grid=(2,),
        in_specs=[rows, rows, projections, projections],
        out_specs=pl.BlockSpec((chips // 2 * tok_rows, 2 * latent_width), lambda i: (i, 0)),
        out_shape=jax.ShapeDtypeStruct((chips * tok_rows, 2 * latent_width), jnp.bfloat16),
        compiler_params=SMALL,
    )(kept, got, kept, got)


def combine_kernel(returned_ref, gates_ref, spread_ref, result_ref):
    latent_width = returned_ref.shape[1] // 2
    count = spread_ref.shape[0]
    gated = dot(gates_ref[...], returned_ref[:, :latent_width])
    result_ref[:, :latent_width] = (gated[:count] + gated[count:]).astype(jnp.bfloat16)
    result_ref[:, latent_width:] = dot(spread_ref[...], returned_ref[:, latent_width:]).astype(
        jnp.bfloat16
    )


def combined_latents(returned, gates, spread):
    return pl.pallas_call(
        combine_kernel,
        out_shape=jax.ShapeDtypeStruct((spread.shape[0], returned.shape[1]), jnp.bfloat16),
        compiler_params=SMALL,
    )(returned, gates, spread)


def share_kernel(pieces_ref, result_ref):
    summed = jnp.sum(pieces_ref[...].astype(jnp.float32), axis=0).astype(jnp.bfloat16)
    result_ref[...] = jnp.broadcast_to(summed[None], result_ref.shape)


def shared_sums(pieces):
    return pl.pallas_call(
        share_kernel,
        out_shape=jax.ShapeDtypeStruct(pieces.shape, jnp.bfloat16),
        compiler_params=SMALL,
    )(pieces)


def dispatch_kernel(latents_ref, spread_ref, gate_ref, result_ref):
    latent_width = latents_ref.shape[1] // 2
    placed = dot(spread_ref[...], latents_ref[...])
    result_ref[:, :latent_width] = placed[:, :latent_width].astype(jnp.bfloat16)
    result_ref[:, latent_width:] = (placed[:, latent_width:] * gate_ref[...]).astype(jnp.bfloat16)


def dispatched_rows(latents, spread, slot_gate):
    return pl.pallas_call(
        dispatch_kernel,
        out_shape=jax.ShapeDtypeStruct((spread.shape[0], latents.shape[1]), jnp.bfloat16),
        compiler_params=SMALL,
    )(latents, spread, slot_gate)


def arrange_kernel(place_ref, *refs):
    *parts, result_ref = refs
    for step, part in enumerate(parts):
        result_ref[lax.rem(place_ref[0] + step, len(parts))] = part[...]


def arranged(place, parts):
    out = jax.ShapeDtypeStruct((len(parts), *parts[0].shape), parts[0].dtype)
    return pl.pallas_call(
        arrange_kernel,
        in_specs=[pl.BlockSpec(memory_space=pltpu.SMEM)]
        + [pl.BlockSpec(memory_space=pltpu.VMEM)] * len(parts),
        out_shape=out,
        compiler_params=SMALL,
    )(place, *parts).reshape(-1, parts[0].shape[1])


def unpack_kernel(scale, packed_ref, down_ref, up_ref):
    features = up_ref.shape[1]
    up_ref[...] = packed_ref[:features].astype(jnp.float32).T * scale
    down_ref[...] = packed_ref[features:].astype(jnp.float32) * scale


def unpack_grads(packed, scale):
    latent_width, features = packed.shape[1], packed.shape[0] // 2
    return pl.pallas_call(
        functools.partial(unpack_kernel, scale),
        out_shape=[
            jax.ShapeDtypeStruct((features, latent_width), jnp.float32),
            jax.ShapeDtypeStruct((latent_width, features), jnp.float32),
        ],
        compiler_params=SMALL,
    )(packed)


def on_device(tokens, cotangent, down_proj, up_proj, routes, gate_weights, expert_in, expert_out):
    expert = ("z", "c")
    chips = lax.axis_size("z")
    core = lax.axis_index("c")
    groups = chips * CORES
    dp_axes = ("y", "x")
    dp = lax.axis_size(dp_axes)
    tok_rows = routes.shape[0]
    group_rows = tokens.shape[0]
    features = tokens.shape[1]
    latent_width = down_proj.shape[1]
    capacity = min(tok_rows, tok_rows * TOPK * 5 // (4 * groups))
    slot_count = groups * capacity
    grad_scale = 1.0 / math.sqrt(group_rows * dp)
    bf16 = jnp.bfloat16

    swap = [(0, 1), (1, 0)]

    blocked = (chips, CORES, tok_rows, features)
    token_blocks = tokens.reshape(blocked)
    cotangent_blocks = cotangent.reshape(blocked)
    place = core.reshape(1).astype(jnp.int32)
    both, place = lax.optimization_barrier((regrouped(expert_in, expert_out, dp), place))
    given, kept = swap_operands(place, token_blocks, cotangent_blocks, down_proj, up_proj)
    got = lax.ppermute(given, "c", swap)
    parts = chip_latents(kept, got, chips, latent_width)
    both, parts = lax.optimization_barrier((both, parts))
    packed = packed_weights(both, expert_out)
    latents = lax.psum_scatter(parts, "z", scatter_dimension=0, tiled=True)

    across = lax.axis_size("x")
    neighbours = [packed]
    for step in range(1, across):
        backward = [(i, (i - step) % across) for i in range(across)]
        neighbours.append(lax.ppermute(packed, "x", backward))
    column = lax.axis_index("x").reshape(1).astype(jnp.int32)
    weights = lax.all_gather(arranged(column, neighbours), "y", axis=0, tiled=True)

    to_slot, slot_gate, to_token, gates = lax.optimization_barrier(
        slot_tables(routes, gate_weights, groups, capacity)
    )

    def exchange(rows):
        return lax.all_to_all(
            rows.reshape(groups, capacity, rows.shape[1]),
            expert,
            split_axis=0,
            concat_axis=0,
            tiled=True,
        ).reshape(slot_count, rows.shape[1])

    outgoing = dispatched_rows(latents, to_slot, slot_gate)
    result = run_expert(exchange(outgoing), weights)
    returned = exchange(result)
    latents = combined_latents(returned, gates, to_token)
    latents = lax.all_gather(latents, expert, axis=0, tiled=True)
    all_out = latents[:, :latent_width]
    all_grad = latents[:, latent_width:]
    up_part_grad = dot(cotangent, all_out, ROWS)
    down_part_grad = dot(tokens, all_grad, ROWS)
    grads = jnp.concatenate([up_part_grad, down_part_grad], axis=0).astype(bf16)
    grads = grads.reshape(dp, 2 * features // dp, latent_width)
    grads = lax.all_to_all(grads, dp_axes, split_axis=0, concat_axis=0, tiled=True)
    mixed = dot(all_out, up_proj).astype(bf16)
    input_grad = dot(all_grad, down_proj, COLS).astype(bf16)
    summed = shared_sums(grads)
    summed = lax.all_to_all(summed, dp_axes, split_axis=0, concat_axis=0, tiled=True)
    down_grad, up_grad = unpack_grads(summed.reshape(2 * features, latent_width), grad_scale)
    return mixed, input_grad, down_grad, up_grad


def solution(mesh):
    dp, experts = mesh.devices.shape
    across = math.gcd(dp, ACROSS)
    shape = (dp // across, across, experts // CORES, CORES)
    fine = Mesh(mesh.devices.reshape(shape), ("y", "x", "z", "c"))
    group = ("y", "x")
    expert = ("z", "c")
    in_specs = (
        P(group, expert),
        P(group, expert),
        P(expert, None),
        P(None, expert),
        P(("y", "x", "z", "c"), None),
        P(("y", "x", "z", "c"), None),
        P(expert, group, None),
        P(expert, group, None),
    )
    out_specs = (P(group, expert), P(group, expert), P(expert, None), P(None, expert))
    return jax.shard_map(
        on_device, mesh=fine, in_specs=in_specs, out_specs=out_specs, check_vma=False
    )
```
